128 devices in a mesh: lat: 16 (over z_lo, x, core), lev: 8 (over y, z_hi).
Axes of the slice: x: 4, y: 4, z: 4 (z_hi: 2, z_lo: 2; z = z_hi * 2 + z_lo), core: 2. Of those that a mesh axis runs over, the one named last changes fastest.
Arguments:
- tracers: float32 [8, 128, 104, 1152], P(None, 'lat', 'lev'), may hold values from -6 to 6
- courant_lon: float32 [128, 104, 1152], P('lat', 'lev'), may hold values from -0.6 to 0.6
- courant_lat: float32 [128, 104, 1152], P('lat', 'lev'), may hold values from -0.6 to 0.6
- level_counts: int32 [8], replicated, may hold values from 1 to 13, 72 in all
- thick_source: float32 [128, 72, 1152], P('lat', None, 'lev'), may hold values from 0.3 to 3
- eta_weights: float32 [72], replicated, may hold values from 0.3 to 3
Outputs:
- remapped: float32 [8, 128, 72, 1152], P(None, 'lat', None, 'lev')
The draws below stay inside these ranges and needn't reach their ends.
Inputs may be any that keep to these rules, and one draw needn't show every extreme that they name: `level_counts`: the level counts sum to 72; the index of lev that holds the most levels holds exactly 13.
All inputs are finite; a program needn't handle non-finite values.
Results may differ from the reference program's by a relative error of at most 0.0003.
Values sent between devices are 32-bit elements; how exact they have to be, the bound alone decides.
A program may use at most 128 MiB of HBM per device.

```python
import math
import jax
import jax.numpy as jnp
import numpy as np
from jax import lax

NLON = 1152
NLEV = 72
NTR = 8
NLAT = 128
LMAX = 13
SLOTS = 104
N_LEV = 8


def level_of(stream_key, extent, shards, low, high):
    def one(position, parts):
        steps = jax.random.uniform(jax.random.fold_in(jax.random.fold_in(stream_key, 6), position), (parts,), jnp.float32, low / len(shards), high / len(shards))
        return jnp.repeat(jnp.exp(steps), extent[position] // parts).reshape((-1,) + (1,) * (len(extent) - position - 1))

    gain = one(*shards[0])
    for cut in shards[1:]:
        gain = gain * one(*cut)
    return gain


def profile(number_of, total, bound, skew):
    loads = [(1 << 20) // math.isqrt(grade ** skew) + 1 for grade in range(2, number_of + 1)]
    rest, holding = total - bound - (number_of - 1), [1] * (number_of - 1)
    while rest > 0:
        candidates = [i for i in range(number_of - 1) if holding[i] < bound]
        mass, remaining = sum([loads[i] for i in candidates]), rest
        for i in candidates:
            more = min(bound - holding[i], max(1, remaining * loads[i] // mass), rest)
            holding[i] = holding[i] + more
            rest = rest - more
    return np.array([bound] + holding)


def ragged(own_key, count, total, most, lean):
    if count == 2:
        one = jax.random.randint(own_key, (), max(1, total - most), min(most, total - 1) + 1)
        return jnp.stack([one, total - one])
    tallies = jnp.asarray(profile(count, total, most, lean), jnp.int32)
    twos = (count - 1) // 2
    giver, receiver = tallies[1:1 + 2 * twos:2], tallies[2:2 + 2 * twos:2]
    room = jnp.minimum(giver - 1, most - receiver)
    passed = jax.random.randint(jax.random.fold_in(own_key, 1), (twos,), 0, 1 << 20) % (room + 1)
    tallies = tallies.at[1:1 + 2 * twos:2].set(giver - passed).at[2:2 + 2 * twos:2].set(receiver + passed)
    return tallies[jax.random.permutation(jax.random.fold_in(own_key, 2), count)]


def bell_draw(own_key, shape, scale, bound, shards=(), kind=jnp.bfloat16):
    entries = scale * jax.random.normal(own_key, shape, jnp.float32)
    if shards:
        entries = entries * level_of(own_key, shape, shards, -0.22, 0.18)
    return jnp.clip(entries, -bound, bound).astype(kind)


def setup_inputs(seed: int = 0) -> dict:
    streams_of = jax.random.split(jax.random.key(seed), 7)
    return {
        "tracers": bell_draw(streams_of[0], (NTR, NLAT, SLOTS, NLON), 1.0, 6.0, ((1, 16), (2, 8)), jnp.float32),
        "courant_lon": jnp.clip(jax.random.uniform(streams_of[1], (NLAT, SLOTS, NLON), jnp.float32, -0.6, 0.6) * level_of(streams_of[1], (NLAT, SLOTS, NLON), ((0, 16), (1, 8)), -0.4, 0.0), -0.6, 0.6),
        "courant_lat": jnp.clip(jax.random.uniform(streams_of[2], (NLAT, SLOTS, NLON), jnp.float32, -0.6, 0.6) * level_of(streams_of[2], (NLAT, SLOTS, NLON), ((0, 16), (1, 8)), -0.4, 0.0), -0.6, 0.6),
        "level_counts": ragged(streams_of[3], N_LEV, NLEV, LMAX, 2).astype(jnp.int32),
        "thick_source": jnp.clip(jnp.exp(math.log(3.0) - 2.3025851 * jax.random.uniform(streams_of[4], (NLAT, NLEV, NLON), jnp.float32) ** level_of(streams_of[4], (NLAT, NLEV, NLON), ((0, 16), (2, 8)), -0.2, 0.2)), 0.3, 3.0),
        "eta_weights": jnp.clip(jnp.exp(jax.random.uniform(streams_of[5], (NLEV,), jnp.float32, math.log(0.3), math.log(3.0))), 0.3, 3.0),
    }


def cut_along(values, begin, finish, axis):
    return lax.slice_in_dim(values, begin, finish, axis=axis)


def ppm_flux(extended, courant, axis):
    length = extended.shape[axis]
    inner = length - 6
    face = (7.0 * (cut_along(extended, 1, length - 2, axis) + cut_along(extended, 2, length - 1, axis))
            - (cut_along(extended, 0, length - 3, axis) + cut_along(extended, 3, length, axis))) / 12.0
    left_edge = cut_along(face, 0, inner + 2, axis)
    right_edge = cut_along(face, 1, inner + 3, axis)
    centre = cut_along(extended, 2, inner + 4, axis)
    slope = right_edge - left_edge
    curve = 6.0 * centre - 3.0 * (left_edge + right_edge)
    amount = -courant
    positive = courant * (cut_along(right_edge, 0, inner + 1, axis) - 0.5 * courant * (
        cut_along(slope, 0, inner + 1, axis) - (1.0 - 2.0 * courant / 3.0) * cut_along(curve, 0, inner + 1, axis)))
    negative = courant * (cut_along(left_edge, 1, inner + 2, axis) + 0.5 * amount * (
        cut_along(slope, 1, inner + 2, axis) + (1.0 - 2.0 * amount / 3.0) * cut_along(curve, 1, inner + 2, axis)))
    return jnp.where(courant >= 0.0, positive, negative)


def slot_table(level_counts, slot_width, levels):
    count_total = level_counts.shape[0]
    starts = (jnp.cumsum(level_counts) - level_counts).astype(jnp.int32)
    level_ids = jnp.arange(levels, dtype=jnp.int32)
    owner = (jnp.sum((starts[None, :] <= level_ids[:, None]).astype(jnp.int32), axis=1) - 1).astype(jnp.int32)
    picked = owner[:, None] == jnp.arange(count_total, dtype=jnp.int32)[None, :]
    owner_start = jnp.sum(jnp.where(picked, starts[None, :], 0), axis=1).astype(jnp.int32)
    return (owner * slot_width + level_ids - owner_start).astype(jnp.int32)


def intersection_weights(thick, eta_weights):
    tops = jnp.cumsum(thick, axis=1)
    zero_row = jnp.zeros_like(thick[:, :1])
    source = jnp.concatenate([zero_row, tops], axis=1)
    surface = tops[:, -1:]
    total = jnp.sum(eta_weights)
    fraction = jnp.cumsum(eta_weights) / total
    target = jnp.concatenate([zero_row, surface * fraction[None, :, None]], axis=1)
    target_thick = surface * (eta_weights / total)[None, :, None]
    upper = jnp.minimum(target[:, 1:, None, :], source[:, None, 1:, :])
    lower = jnp.maximum(target[:, :-1, None, :], source[:, None, :-1, :])
    return jnp.maximum(upper - lower, 0.0) / target_thick[:, :, None, :]


def apply_remap(weights, columns):
    return jnp.einsum("rkjw,trjw->trkw", weights, columns, precision=lax.Precision.HIGHEST)


def reference(tracers, courant_lon, courant_lat, level_counts, thick_source, eta_weights):
    lon_faces = jnp.concatenate([courant_lon, courant_lon[:, :, :1]], axis=2)
    lat_padded = jnp.pad(courant_lat, ((3, 3), (0, 0), (0, 0)))
    lat_faces = lat_padded[3:NLAT + 4]

    def horizontal_one(field):
        along_lon = jnp.concatenate([field[:, :, -3:], field, field[:, :, :3]], axis=2)
        flux_lon = ppm_flux(along_lon, lon_faces, 2)
        along_lat = jnp.pad(field, ((3, 3), (0, 0), (0, 0)))
        flux_lat = ppm_flux(along_lat, lat_faces, 0)
        return field - (flux_lon[:, :, 1:] - flux_lon[:, :, :-1]) - (flux_lat[1:] - flux_lat[:-1])

    horizontal = lax.map(horizontal_one, tracers)
    slots = slot_table(level_counts, LMAX, NLEV)
    columns = jnp.take(horizontal, slots, axis=2)

    def remap_row(pair):
        row_columns, row_thick = pair
        weights = intersection_weights(row_thick[None], eta_weights)
        return apply_remap(weights, row_columns[:, None])[:, 0]

    remapped = lax.map(remap_row, (jnp.moveaxis(columns, 1, 0), thick_source))
    return jnp.moveaxis(remapped, 0, 1)
```

```python
import functools
import jax
import jax.numpy as jnp
from jax import lax
from jax.experimental import pallas as pl
from jax.experimental.pallas import tpu as pltpu
from jax.sharding import PartitionSpec as P

MESH = pl.DeviceIdType.MESH
HI = lax.Precision.HIGHEST
F32 = jnp.float32
NT, NI, NS, NX, ND = 8, 8, 13, 1152, 8
SPAN = NX // ND
ROWS = 120


def gather8(v, idx):
    return jnp.take_along_axis(v, idx, axis=0, mode="promise_in_bounds")


def face_weights(c):
    m = jnp.abs(c)
    r = 1.0 - m
    cm = c * m
    return c * r * r * (1.0 / 12.0), cm * (3.0 - 2.0 * m), cm * r * (-1.0 / 12.0)


def latitude_part(t, xs, south, north, wlat, part):
    def column(k, _):
        lanes = pl.ds(pl.multiple_of(k * 128, 128), 128)
        for lo, hi in ((0, 8), (8, NS)):
            q = [south[t, j, lo:hi, lanes] for j in range(3)]
            q += [xs[t, j, lo:hi, lanes] for j in range(NI)]
            q += [north[t, j, lo:hi, lanes] for j in range(3)]
            a = [7.0 * (q[j + 1] + q[j + 2]) - (q[j] + q[j + 3]) for j in range(NI + 3)]
            before = None
            for f in range(NI + 1):
                w0 = wlat[0, f, lo:hi, lanes]
                up = w0 >= 0.0
                flux = (
                    w0 * a[f + 1]
                    + wlat[1, f, lo:hi, lanes] * jnp.where(up, q[f + 2], q[f + 3])
                    + wlat[2, f, lo:hi, lanes] * jnp.where(up, a[f], a[f + 2])
                )
                if f > 0:
                    part[f - 1, lo:hi, lanes] = q[f + 2] - (flux - before)
                before = flux
        return 0

    lax.fori_loop(0, NX // 128, column, 0)


def longitude_part(t, xs, wlon, part, send):
    for i in range(NI):
        for lo, hi in ((0, 8), (8, NS)):
            q = xs[t, i, lo:hi, :]
            west = jnp.roll(q, 1, axis=1)
            a = 7.0 * (west + q) - (jnp.roll(q, 2, axis=1) + jnp.roll(q, -1, axis=1))
            w0 = wlon[0, i, lo:hi, :]
            up = w0 >= 0.0
            flux = (
                w0 * a
                + wlon[1, i, lo:hi, :] * jnp.where(up, west, q)
                + wlon[2, i, lo:hi, :] * jnp.where(up, jnp.roll(a, 1, axis=1), jnp.roll(a, -1, axis=1))
            )
            h = part[i, lo:hi, :] - (jnp.roll(flux, -1, axis=1) - flux)
            n = hi - lo
            base = n * i if lo == 0 else 72 + n * i
            tail = 64 if lo == 0 else 112
            for e in range(ND):
                send[t, e, base:base + n, :] = h[:, SPAN * e:SPAN * e + 128]
                send[t, e, tail:tail + n, 16 * i:16 * i + 16] = h[:, SPAN * e + 128:SPAN * e + SPAN]


def prep(cnt_ref, thick_ref, eta_ref, sl_s, h_s, idx_s, dt_s, rt_s, fr_s, th_s):
    for i in range(8):
        th_s[i] = thick_ref[i, :, 0:128]
        th_s[8, :, 16 * i:16 * i + 16] = thick_ref[i, :, 128:144]
    rows = lax.broadcasted_iota(jnp.int32, (128, 128), 0)
    lanes = lax.broadcasted_iota(jnp.int32, (128, 128), 1)
    dd, ss = rows >> 4, rows & 15
    hi = jnp.zeros((128, 128), jnp.int32)
    lo = jnp.zeros((128, 128), jnp.int32)
    start = jnp.int32(0)
    for d in range(8):
        c = cnt_ref[d]
        hi = jnp.where(dd == d, start + jnp.minimum(ss + 1, c), hi)
        lo = jnp.where(dd == d, start + jnp.minimum(ss, c), lo)
        start = start + c
    mu = jnp.where(lanes < hi, 1.0, 0.0)[:, :72]
    ml = jnp.where(lanes < lo, 1.0, 0.0)[:, :72]
    er = eta_ref[...]
    r72 = lax.broadcasted_iota(jnp.int32, (72, 72), 0)
    l72 = lax.broadcasted_iota(jnp.int32, (72, 72), 1)
    eb = jnp.broadcast_to(er, (72, 72))
    tot = jnp.sum(eb, axis=1, keepdims=True)
    cum = jnp.sum(jnp.where(l72 <= r72, eb, 0.0), axis=1, keepdims=True)
    own = jnp.sum(jnp.where(l72 == r72, eb, 0.0), axis=1, keepdims=True)
    fr_s[0] = jnp.broadcast_to(cum / tot, (72, 128))
    fr_s[1] = jnp.broadcast_to(own / tot, (72, 128))

    def one(ct, _):
        th = th_s[ct]
        su = jnp.dot(mu, th, precision=HI, preferred_element_type=jnp.float32)
        sl = jnp.dot(ml, th, precision=HI, preferred_element_type=jnp.float32)
        sl_s[0] = sl
        sl_s[1] = su
        h_s[ct] = su - sl
        ps = jnp.broadcast_to(su[127:128, :], (8, 128))
        for tb in range(9):
            t = ps * fr_s[0, 8 * tb:8 * tb + 8, :]
            rt_s[ct, 8 * tb:8 * tb + 8, :] = 1.0 / (ps * fr_s[1, 8 * tb:8 * tb + 8, :])
            n = jnp.zeros((8, 128), jnp.int32)
            for d in range(8):
                for s in range(13):
                    row = jnp.broadcast_to(sl_s[1, 16 * d + s:16 * d + s + 1, :], (8, 128))
                    n = n + jnp.where(row <= t, 1 + (3 if s == 12 else 0), 0)
            n = jnp.minimum(n, 127)
            loc = n & 7
            vb = n >> 3
            g = jnp.zeros((8, 128), jnp.float32)
            gh = jnp.zeros((8, 128), jnp.float32)
            for v in range(16):
                hit = vb == v
                g = jnp.where(hit, gather8(sl_s[0, 8 * v:8 * v + 8, :], loc), g)
                gh = jnp.where(hit, gather8(h_s[ct, 8 * v:8 * v + 8, :], loc), gh)
            idx_s[ct, 8 * tb:8 * tb + 8, :] = n
            dt_s[ct, 8 * tb:8 * tb + 8, :] = jnp.clip(t - g, 0.0, gh)
        return 0
    lax.fori_loop(0, 9, one, 0)

def remap_tile(q_of, ct, h_s, idx_s, dt_s, rt_s, c_s, q_s, f_s, tri):
    for d in range(8):
        a, b = q_of(d)
        q_s[16 * d:16 * d + 8, :] = a
        q_s[16 * d + 8:16 * d + 16, :] = b
    q = q_s[...]
    c_s[...] = jnp.dot(tri, h_s[ct] * q, precision=HI, preferred_element_type=jnp.float32)
    f_s[0:8, :] = jnp.zeros((8, 128), jnp.float32)
    for tb in range(9):
        n = idx_s[ct, 8 * tb:8 * tb + 8, :]
        loc, vb = n & 7, n >> 3
        gc = jnp.zeros((8, 128), jnp.float32)
        gq = jnp.zeros((8, 128), jnp.float32)
        for v in range(16):
            hit = vb == v
            gc = jnp.where(hit, gather8(c_s[8 * v:8 * v + 8, :], loc), gc)
            gq = jnp.where(hit, gather8(q_s[8 * v:8 * v + 8, :], loc), gq)
        f_s[8 + 8 * tb:16 + 8 * tb, :] = gc + dt_s[ct, 8 * tb:8 * tb + 8, :] * gq
    return (f_s[8:80, :] - f_s[7:79, :]) * rt_s[ct]


def kernel(lat_axis, lev_axis, cnt_ref, x_hbm, clon_hbm, clat_hbm, thick_hbm, eta_ref, out_hbm,
           xs, south, north, clon, clat, cnorth, wlat, wlon, part, send, recv, thick, stage,
           sl_s, h_s, idx_s, dt_s, rt_s, fr_s, th_s, c_s, q_s, f_s,
           x_sem, c_sem, hsend, hrecv, ssem, rsem, lsem, osem):
    lat, lev = lax.axis_index("lat"), lax.axis_index("lev")

    loads = [pltpu.make_async_copy(x_hbm.at[t], xs.at[t], x_sem.at[t]) for t in range(NT)]
    small = [pltpu.make_async_copy(clat_hbm, clat, c_sem.at[0]), pltpu.make_async_copy(clon_hbm, clon, c_sem.at[1]),
             pltpu.make_async_copy(thick_hbm, thick, c_sem.at[2])]
    small[0].start()
    loads[0].start()
    small[1].start()
    for c in loads[1:]:
        c.start()
    small[2].start()

    def peer(k):
        return lax.rem(lev + k, ND)

    bar = pltpu.get_barrier_semaphore()
    for k in range(1, ND):
        pl.semaphore_signal(bar, inc=1, device_id=(lat, peer(k)), device_id_type=MESH)

    @pl.when(lat > 0)
    def _():
        pl.semaphore_signal(bar, inc=1, device_id=(lat - 1, lev), device_id_type=MESH)

    @pl.when(lat < lat_axis - 1)
    def _():
        pl.semaphore_signal(bar, inc=1, device_id=(lat + 1, lev), device_id_type=MESH)

    inner = jnp.where(lat > 0, 1, 0) + jnp.where(lat < lat_axis - 1, 1, 0)
    pl.semaphore_wait(bar, ND - 1 + inner)

    def edge_copy():
        return pltpu.make_async_remote_copy(clat_hbm.at[0], cnorth, hsend.at[2, 0], hrecv.at[2, 0],
                                            device_id=(lat - 1, lev), device_id_type=MESH)

    def to_south(t):
        return pltpu.make_async_remote_copy(x_hbm.at[t, 0:3], north.at[t], hsend.at[0, t], hrecv.at[0, t],
                                            device_id=(lat - 1, lev), device_id_type=MESH)

    def to_north(t):
        return pltpu.make_async_remote_copy(x_hbm.at[t, NI - 3:NI], south.at[t], hsend.at[1, t], hrecv.at[1, t],
                                            device_id=(lat + 1, lev), device_id_type=MESH)

    has_south, has_north = lat > 0, lat < lat_axis - 1

    @pl.when(has_south)
    def _():
        edge_copy().start()

    for t in range(NT):
        @pl.when(has_south)
        def _():
            to_south(t).start()

        @pl.when(has_north)
        def _():
            to_north(t).start()

    @pl.when(lat == 0)
    def _():
        south[...] = jnp.zeros_like(south)

    @pl.when(lat == lat_axis - 1)
    def _():
        north[...] = jnp.zeros_like(north)
        cnorth[...] = jnp.zeros_like(cnorth)

    small[0].wait()
    small[1].wait()

    def weigh(i, _):
        for k, w in enumerate(face_weights(clat[i])):
            wlat[k, i] = w
        for k, w in enumerate(face_weights(clon[i])):
            wlon[k, i] = w
        return 0

    lax.fori_loop(0, NI, weigh, 0)

    def clear(t, _):
        for e in range(ND):
            send[t, e, 112:120, :] = jnp.zeros((8, 128), F32)
        return 0

    lax.fori_loop(0, NT, clear, 0)

    @pl.when(has_north)
    def _():
        edge_copy().wait_recv()

    for k, w in enumerate(face_weights(cnorth[...])):
        wlat[k, NI] = w

    def across(t, k):
        e = peer(k)
        return pltpu.make_async_remote_copy(send.at[t, e], recv.at[lev, t], ssem.at[t, k], rsem.at[t, lev],
                                            device_id=(lat, e), device_id_type=MESH)

    def own(t):
        return pltpu.make_async_copy(send.at[t, lev], recv.at[lev, t], lsem.at[t])

    def forward(t, _):
        pltpu.make_async_copy(x_hbm.at[t], xs.at[t], x_sem.at[t]).wait()

        @pl.when(has_north)
        def _():
            to_south(t).wait_recv()

        @pl.when(has_south)
        def _():
            to_north(t).wait_recv()

        latitude_part(t, xs, south, north, wlat, part)
        longitude_part(t, xs, wlon, part, send)
        for k in ORDER:
            across(t, k).start()
        own(t).start()
        return 0

    lax.fori_loop(0, NT, forward, 0)

    small[2].wait()
    prep(cnt_ref, thick, eta_ref, sl_s, h_s, idx_s, dt_s, rt_s, fr_s, th_s)

    r = lax.broadcasted_iota(jnp.int32, (128, 128), 0)
    l = lax.broadcasted_iota(jnp.int32, (128, 128), 1)
    tri = jnp.where(l < r, 1.0, 0.0)

    def put(t, slot):
        return pltpu.make_async_copy(stage.at[slot], out_hbm.at[t], osem.at[slot])

    def settle(t, _):
        slot = lax.rem(t, 2)

        @pl.when(t >= 2)
        def _():
            put(t - 2, slot).wait()

        own(t).wait()
        for k in range(1, ND):
            src = peer(k)
            pltpu.make_async_remote_copy(send.at[t, src], recv.at[src, t], ssem.at[t, k], rsem.at[t, src],
                                         device_id=(lat, src), device_id_type=MESH).wait_recv()

        def tile(ct, _):
            def q_of(d):
                return recv[d, t, pl.ds(pl.multiple_of(8 * ct, 8), 8), :], recv[d, t, pl.ds(72 + 5 * ct, 8), :]
            res = remap_tile(q_of, ct, h_s, idx_s, dt_s, rt_s, c_s, q_s, f_s, tri)

            @pl.when(ct < NI)
            def _():
                stage[slot, lax.rem(ct, NI), :, 0:128] = res

            @pl.when(ct == NI)
            def _():
                for i in range(NI):
                    stage[slot, i, :, 128:SPAN] = res[:, 16 * i:16 * i + 16]
            return 0

        lax.fori_loop(0, NI + 1, tile, 0)
        put(t, slot).start()
        return 0

    lax.fori_loop(0, NT, settle, 0)
    put(NT - 2, 0).wait()
    put(NT - 1, 1).wait()

    def drain(t, _):
        for k in range(1, ND):
            across(t, k).wait_send()

        @pl.when(has_south)
        def _():
            to_south(t).wait_send()

        @pl.when(has_north)
        def _():
            to_north(t).wait_send()
        return 0

    lax.fori_loop(0, NT, drain, 0)

    @pl.when(has_south)
    def _():
        edge_copy().wait_send()


ORDER = (1, 7, 2, 6, 3, 5, 4)


def shards(tracers, courant_lon, courant_lat, level_counts, thick_source, eta_weights):
    dma, any_ = pltpu.SemaphoreType.DMA, pl.BlockSpec(memory_space=pl.ANY)
    lat_axis, lev_axis = lax.axis_size("lat"), lax.axis_size("lev")
    return pl.pallas_call(
        functools.partial(kernel, lat_axis, lev_axis),
        name="transport",
        out_shape=jax.ShapeDtypeStruct((NT, NI, 72, SPAN), F32),
        in_specs=[pl.BlockSpec(memory_space=pltpu.SMEM), any_, any_, any_, any_, pl.BlockSpec(memory_space=pltpu.VMEM)],
        out_specs=any_,
        scratch_shapes=[
            pltpu.VMEM((NT, NI, NS, NX), F32),
            pltpu.VMEM((NT, 3, NS, NX), F32),
            pltpu.VMEM((NT, 3, NS, NX), F32),
            pltpu.VMEM((NI, NS, NX), F32),
            pltpu.VMEM((NI, NS, NX), F32),
            pltpu.VMEM((NS, NX), F32),
            pltpu.VMEM((3, NI + 1, NS, NX), F32),
            pltpu.VMEM((3, NI, NS, NX), F32),
            pltpu.VMEM((NI, NS, NX), F32),
            pltpu.VMEM((NT, ND, ROWS, 128), F32),
            pltpu.VMEM((ND, NT, ROWS, 128), F32),
            pltpu.VMEM((NI, 72, SPAN), F32),
            pltpu.VMEM((2, NI, 72, SPAN), F32),
            pltpu.VMEM((2, 128, 128), F32),
            pltpu.VMEM((9, 128, 128), F32),
            pltpu.VMEM((9, 72, 128), jnp.int32),
            pltpu.VMEM((9, 72, 128), F32),
            pltpu.VMEM((9, 72, 128), F32),
            pltpu.VMEM((2, 72, 128), F32),
            pltpu.VMEM((9, 72, 128), F32),
            pltpu.VMEM((128, 128), F32),
            pltpu.VMEM((128, 128), F32),
            pltpu.VMEM((80, 128), F32),
            dma((NT,)),
            dma((3,)),
            dma((3, NT)),
            dma((3, NT)),
            dma((NT, ND)),
            dma((NT, ND)),
            dma((NT,)),
            dma((2,)),
        ],
        compiler_params=pltpu.CompilerParams(collective_id=0, has_side_effects=True, vmem_limit_bytes=52 << 20),
    )(level_counts, tracers, courant_lon, courant_lat, thick_source, eta_weights.reshape(1, 72))


def solution(mesh):
    return jax.shard_map(
        shards,
        mesh=mesh,
        in_specs=(
            P(None, "lat", "lev", None),
            P("lat", "lev", None),
            P("lat", "lev", None),
            P(),
            P("lat", None, "lev"),
            P(),
        ),
        out_specs=P(None, "lat", None, "lev"),
        check_vma=False,
    )
```

```python
import functools
import jax
import jax.numpy as jnp
from jax import lax
from jax.experimental import pallas as pl
from jax.experimental.pallas import tpu as pltpu
from jax.sharding import PartitionSpec as P

MESH = pl.DeviceIdType.MESH
HI = lax.Precision.HIGHEST
F32 = jnp.float32
NT, NI, NS, NX, ND, NK = 8, 8, 13, 1152, 8, 72
SPAN = NX // ND
ROWS = 120
SLOTS = ND * NS
ORDER = (1, 7, 2, 6, 3, 5, 4)


def gather(v, idx, axis):
    return jnp.take_along_axis(v, idx, axis=axis, mode="promise_in_bounds")


def iota(shape, axis):
    return lax.broadcasted_iota(jnp.int32, shape, axis)


def face_weights(c):
    m = jnp.abs(c)
    r = 1.0 - m
    cm = c * m
    return c * r * r * (1.0 / 12.0), cm * (3.0 - 2.0 * m), cm * r * (-1.0 / 12.0)


def flux_of(w, a, behind, ahead, a_behind, a_ahead):
    up = w[0] >= 0.0
    return w[0] * a + w[1] * jnp.where(up, behind, ahead) + w[2] * jnp.where(up, a_behind, a_ahead)


def face(q2, q1, q, qa):
    return 7.0 * (q1 + q) - (q2 + qa)


def edges(t, rows, inner, wedge, edge_s):
    def column(k, _):
        lanes = pl.ds(pl.multiple_of(k * 128, 128), 128)
        for lo, hi in ((0, 8), (8, NS)):
            n0, n1, n2, s3, s2, s1 = [rows[t, j, lo:hi, lanes] for j in range(6)]
            q0, q5, q6, q7 = [inner[t, j, lo:hi, lanes] for j in range(4)]
            a8 = face(q6, q7, n0, n1)
            edge_s[0, lo:hi, lanes] = face(s3, s2, s1, q0)
            edge_s[1, lo:hi, lanes] = a8
            edge_s[2, lo:hi, lanes] = flux_of(
                [wedge[j, lo:hi, lanes] for j in range(3)], a8, q7, n0, face(q5, q6, q7, n0), face(q7, n0, n1, n2))
        return 0

    lax.fori_loop(0, NX // 128, column, 0)


def stencil():
    p, c = iota((4 * 128, 4 * 128), 0), iota((4 * 128, 4 * 128), 1)
    u, kind = p & 127, c >> 7
    at = jnp.where(p < 256, u, jnp.where(u >= 64, u - 128, u + 128)) - (c & 127)
    near = at + jnp.where(kind == 1, 1, jnp.where(kind == 2, -1, 0))
    value = jnp.where((near == -1) | (near == 0), 7.0, jnp.where((near == -2) | (near == 1), -1.0, 0.0))
    return jnp.where(kind == 3, jnp.where(at == -1, 1.0, 0.0), value).astype(jnp.bfloat16)


def halves(v):
    hi = v.astype(jnp.bfloat16)
    return hi, (v - hi.astype(F32)).astype(jnp.bfloat16)


def lane_stencil(t, xs, sten, taps, faces):
    nk = NX // 128
    pad = jnp.zeros((8, 128), F32)
    lane = iota((NS * NI, 128), 1)
    for k in range(nk):
        col = [xs[t, :, :, 128 * j:128 * j + 128].reshape(NS * NI, 128) for j in ((k + nk - 1) % nk, k, (k + 1) % nk)]
        both = halves(jnp.concatenate([col[1], pad], axis=0)) + halves(
            jnp.concatenate([jnp.where(lane >= 64, col[0], col[2]), pad], axis=0))
        for j, piece in enumerate(both):
            taps[112 * k:112 * k + 112, 128 * j:128 * j + 128] = piece
    faces[...] = jnp.dot(taps[...], sten[...], preferred_element_type=F32)


def horizontal(t, xs, rows, edge_s, wlat, wlon, sten, taps, faces, send):
    sub, lane = iota((8, 128), 0), iota((8, 128), 1)
    first, second, last = sub == 0, sub == 1, sub == 7
    nk = NX // 128
    lane_stencil(t, xs, sten, taps, faces)

    def wide(ref, l, k):
        return jnp.broadcast_to(ref[l:l + 1, 128 * k:128 * k + 128], (8, 128))

    for l in range(NS):
        q = [xs[t, l, :, 128 * k:128 * k + 128] for k in range(nk)]
        flux = []
        for k in range(nk):
            a, a_west, a_east, west = [faces[112 * k + 8 * l:112 * k + 8 * l + 8, 128 * j:128 * j + 128] for j in range(4)]
            flux.append(flux_of([wlon[j, l, :, 128 * k:128 * k + 128] for j in range(3)], a, west, q[k], a_west, a_east))
        turned = [pltpu.roll(f, 127, 1) for f in flux]
        h = []
        for k in range(nk):
            s1 = wide(rows.at[t, 5], l, k)
            q1 = jnp.where(first, s1, pltpu.roll(q[k], 1, 0))
            q2 = jnp.where(first, wide(rows.at[t, 4], l, k), jnp.where(second, s1, pltpu.roll(q[k], 2, 0)))
            qa = jnp.where(last, wide(rows.at[t, 0], l, k), pltpu.roll(q[k], 7, 0))
            b = face(q2, q1, q[k], qa)
            b1 = jnp.where(first, wide(edge_s.at[0], l, k), pltpu.roll(b, 1, 0))
            ba = jnp.where(last, wide(edge_s.at[1], l, k), pltpu.roll(b, 7, 0))
            g = flux_of([wlat[j, l, :, 128 * k:128 * k + 128] for j in range(3)], b, q1, q[k], b1, ba)
            ga = jnp.where(last, wide(edge_s.at[2], l, k), pltpu.roll(g, 7, 0))
            flux_east = jnp.where(lane < 127, turned[k], turned[(k + 1) % nk])
            h.append((q[k] - (flux_east - flux[k])) - (ga - g))
        tail, at = 104 + 8 * (l // 8), 16 * (l % 8)
        for e in range(ND):
            send[t, e, 8 * l:8 * l + 8, :] = jnp.where(lane >= 16 * e, h[e], h[e + 1]) if e else h[0]
            turn = (128 - 16 * e + at) % 128
            piece = pltpu.roll(h[e + 1], turn, 1) if turn else h[e + 1]
            send[t, e, tail:tail + 8, at:at + 16] = piece[:, at:at + 16]


def split(v, parts):
    out = []
    for _ in range(parts):
        p = v.astype(jnp.bfloat16)
        out.append(p)
        v = v - p.astype(F32)
    return jnp.concatenate(out, axis=0)


def zero_one(mask, parts):
    return jnp.concatenate([jnp.where(mask, 1.0, 0.0)] * parts, axis=1)


def mul(m, v):
    return jnp.dot(m.astype(jnp.bfloat16), v, preferred_element_type=F32)


def prep(lev, cnt_ref, thick_ref, eta_ref, pick_s, sum_s, su_s, th_s, idx_s, dt_s, rt_s, fr_s):
    for i in range(NI):
        th_s[:, 128 * i:128 * i + 128] = pltpu.roll(thick_ref[i, :, 0:128], lax.rem(16 * lev, 128), 1)
        th_s[:, NX - 128 + 16 * i:NX - 112 + 16 * i] = thick_ref[i, :, 128:SPAN]
    level, slot = iota((NK, SLOTS), 0), iota((NK, SLOTS), 1)
    source = jnp.zeros((NK, SLOTS), jnp.int32)
    start = jnp.int32(0)
    for d in range(ND):
        c = cnt_ref[d]
        source = jnp.where((level >= start) & (level < start + c), level - start + NS * d, source)
        start = start + c
    pick_s[...] = zero_one(source == slot, 2)
    sum_s[...] = zero_one(iota((NK + 8, NK), 1) < iota((NK + 8, NK), 0), 2)
    r72, l72 = iota((NK, NK), 0), iota((NK, NK), 1)
    eb = jnp.broadcast_to(eta_ref[...], (NK, NK))
    tot = jnp.sum(eb, axis=1, keepdims=True)
    cum = jnp.sum(jnp.where(l72 <= r72, eb, 0.0), axis=1, keepdims=True)
    own = jnp.sum(jnp.where(l72 == r72, eb, 0.0), axis=1, keepdims=True)
    fr_s[0] = jnp.broadcast_to(cum / tot, (NK, 128))
    fr_s[1] = jnp.broadcast_to(own / tot, (NK, 128))
    su_s[...] = mul(zero_one(iota((NK + 8, NK), 1) < iota((NK + 8, NK), 0), 3), split(th_s[...], 3))

    def one(ct, _):
        lanes = pl.ds(pl.multiple_of(ct * 128, 128), 128)
        ps = jnp.broadcast_to(su_s[NK:NK + 1, lanes], (8, 128))
        for tb in range(NK // 8):
            at = slice(8 * tb, 8 * tb + 8)
            t = ps * fr_s[0, at, :]
            rt_s[ct, at, :] = 1.0 / (ps * fr_s[1, at, :])
            n = jnp.zeros((8, 128), jnp.int32)
            for r in range(NK):
                n = jnp.where(jnp.broadcast_to(su_s[r + 1:r + 2, lanes], (8, 128)) <= t, r + 1, n)
            loc, vb = n & 7, n >> 3
            g = ps
            gh = jnp.zeros((8, 128), F32)
            for v in range(NK // 8):
                hit = vb == v
                g = jnp.where(hit, gather(su_s[8 * v:8 * v + 8, lanes], loc, 0), g)
                gh = jnp.where(hit, gather(th_s[8 * v:8 * v + 8, lanes], loc, 0), gh)
            idx_s[ct, at, :] = n
            dt_s[ct, at, :] = jnp.clip(t - g, 0.0, gh)
        return 0

    lax.fori_loop(0, NI + 1, one, 0)


def block_turn(p):
    r, l = iota((8, 128), 0), iota((8, 128), 1)
    p = gather(p, (l + 16 * r) & 127, 1)
    p = gather(p, (r - (l >> 4)) & 7, 0)
    return gather(p, ((16 * r - (l & 112)) & 127) + (l & 15), 1)


def remap_tracer(lev, t, slot, recv, stage, pick_s, sum_s, th_s, idx_s, dt_s, rt_s, s_s, q_s, c_s, f_s):
    for d in range(ND):
        a, b = slice(NS * d, NS * d + 8), slice(NS * d + 8, NS * d + NS)
        for ct in range(NI):
            lanes = slice(128 * ct, 128 * ct + 128)
            s_s[a, lanes] = recv[d, t, pl.ds(ct, 8, stride=8), :]
            s_s[b, lanes] = recv[d, t, pl.ds(64 + ct, NS - 8, stride=8), :]
        s_s[a, NX - 128:] = block_turn(recv[d, t, 104:112, :])
        s_s[b, NX - 128:] = block_turn(recv[d, t, 112:120, :])[:NS - 8]
    q_s[...] = mul(pick_s[...], split(s_s[...], 2))
    c_s[...] = mul(sum_s[...], split(q_s[...] * th_s[...], 2))
    f_s[0:8, :] = jnp.zeros((8, 128), F32)

    def tile(ct):
        lanes = pl.ds(ct * 128, 128) if isinstance(ct, int) else pl.ds(pl.multiple_of(ct * 128, 128), 128)
        total = jnp.broadcast_to(c_s[NK:NK + 1, lanes], (8, 128))
        for tb in range(NK // 8):
            at = slice(8 * tb, 8 * tb + 8)
            n = idx_s[ct, at, :]
            loc, vb = n & 7, n >> 3
            gc = total
            gq = jnp.zeros((8, 128), F32)
            for v in range(NK // 8):
                hit = vb == v
                gc = jnp.where(hit, gather(c_s[8 * v:8 * v + 8, lanes], loc, 0), gc)
                gq = jnp.where(hit, gather(q_s[8 * v:8 * v + 8, lanes], loc, 0), gq)
            f_s[8 + 8 * tb:16 + 8 * tb, :] = gc + dt_s[ct, at, :] * gq
        return (f_s[8:80, :] - f_s[7:79, :]) * rt_s[ct]

    def main(ct, _):
        stage[slot, ct, :, 0:128] = pltpu.roll(tile(ct), lax.rem(128 - 16 * lev, 128), 1)
        return 0

    lax.fori_loop(0, NI, main, 0)
    res = tile(NI)
    for i in range(NI):
        stage[slot, i, :, 128:SPAN] = res[:, 16 * i:16 * i + 16]


def kernel(lat_axis, cnt_ref, x_hbm, clon_hbm, clat_hbm, thick_ref, eta_ref, out_ref,
           xs, rows, inner, clon, clat, cnorth, wlat, wedge, wlon, edge_s, sten, taps, faces, send, recv,
           pick_s, sum_s, su_s, th_s, idx_s, dt_s, rt_s, fr_s, s_s, q_s, c_s, f_s,
           x_sem, i_sem, c_sem, esem, hsend, hrecv, ssem, rsem, lsem):
    lat, lev = lax.axis_index("lat"), lax.axis_index("lev")
    has_south, has_north = lat > 0, lat < lat_axis - 1

    small = [pltpu.make_async_copy(clat_hbm, clat, c_sem.at[0]), pltpu.make_async_copy(clon_hbm, clon, c_sem.at[1])]
    loads = [pltpu.make_async_copy(x_hbm.at[t], xs.at[t], x_sem.at[t]) for t in range(NT)]
    def inner_load(t, j):
        return pltpu.make_async_copy(x_hbm.at[t, :, (0, 5, 6, 7)[j], :], inner.at[t, j], i_sem.at[t, j])

    small[0].start()
    small[1].start()
    for t in range(NT):
        loads[t].start()
        for j in range(4):
            inner_load(t, j).start()

    def peer(k):
        return lax.rem(lev + k, ND)

    bar = pltpu.get_barrier_semaphore()
    for k in range(1, ND):
        pl.semaphore_signal(bar, inc=1, device_id=(lat, peer(k)), device_id_type=MESH)

    @pl.when(has_south)
    def _():
        pl.semaphore_signal(bar, inc=1, device_id=(lat - 1, lev), device_id_type=MESH)

    @pl.when(has_north)
    def _():
        pl.semaphore_signal(bar, inc=1, device_id=(lat + 1, lev), device_id_type=MESH)

    others = jnp.where(has_south, 1, 0) + jnp.where(has_north, 1, 0)
    pl.semaphore_wait(bar, ND - 1 + others)

    def edge_copy():
        return pltpu.make_async_remote_copy(clat_hbm.at[:, 0, :], cnorth, esem.at[0], esem.at[1],
                                            device_id=(lat - 1, lev), device_id_type=MESH)

    def to_south(t, j):
        return pltpu.make_async_remote_copy(x_hbm.at[t, :, j, :], rows.at[t, j], hsend.at[t, j], hrecv.at[t, j],
                                            device_id=(lat - 1, lev), device_id_type=MESH)

    def to_north(t, j):
        return pltpu.make_async_remote_copy(x_hbm.at[t, :, 2 + j, :], rows.at[t, j], hsend.at[t, j], hrecv.at[t, j],
                                            device_id=(lat + 1, lev), device_id_type=MESH)

    @pl.when(has_south)
    def _():
        edge_copy().start()

    for t in range(NT):
        @pl.when(has_south)
        def _():
            for j in range(3):
                to_south(t, j).start()

        @pl.when(has_north)
        def _():
            for j in range(3, 6):
                to_north(t, j).start()

    @pl.when(lat == 0)
    def _():
        rows[:, 3:6] = jnp.zeros((NT, 3, NS, NX), F32)

    @pl.when(lat == lat_axis - 1)
    def _():
        rows[:, 0:3] = jnp.zeros((NT, 3, NS, NX), F32)
        cnorth[...] = jnp.zeros_like(cnorth)

    sten[...] = stencil()
    small[0].wait()
    small[1].wait()

    def weigh(l, _):
        for k, w in enumerate(face_weights(clat[l])):
            wlat[k, l] = w
        for k, w in enumerate(face_weights(clon[l])):
            wlon[k, l] = w
        return 0

    lax.fori_loop(0, NS, weigh, 0)

    def clear(t, _):
        for e in range(ND):
            send[t, e, 112:120, :] = jnp.zeros((8, 128), F32)
        return 0

    lax.fori_loop(0, NT, clear, 0)

    @pl.when(has_north)
    def _():
        edge_copy().wait_recv()

    for k, w in enumerate(face_weights(cnorth[...])):
        wedge[k] = w

    def across(t, k):
        e = peer(k)
        return pltpu.make_async_remote_copy(send.at[t, e], recv.at[lev, t], ssem.at[t, k], rsem.at[t, lev],
                                            device_id=(lat, e), device_id_type=MESH)

    def own(t):
        return pltpu.make_async_copy(send.at[t, lev], recv.at[lev, t], lsem.at[t])

    def forward(t, _):
        pltpu.make_async_copy(x_hbm.at[t], xs.at[t], x_sem.at[t]).wait()

        @pl.when(has_north)
        def _():
            for j in range(3):
                to_south(t, j).wait_recv()

        @pl.when(has_south)
        def _():
            for j in range(3, 6):
                to_north(t, j).wait_recv()

        for j in range(4):
            inner_load(t, j).wait()
        edges(t, rows, inner, wedge, edge_s)
        horizontal(t, xs, rows, edge_s, wlat, wlon, sten, taps, faces, send)
        for k in ORDER:
            across(t, k).start()
        own(t).start()
        return 0

    lax.fori_loop(0, NT, forward, 0)

    prep(lev, cnt_ref, thick_ref, eta_ref, pick_s, sum_s, su_s, th_s, idx_s, dt_s, rt_s, fr_s)

    def settle(t, _):
        own(t).wait()
        for k in range(1, ND):
            src = peer(k)
            pltpu.make_async_remote_copy(send.at[t, src], recv.at[src, t], ssem.at[t, k], rsem.at[t, src],
                                         device_id=(lat, src), device_id_type=MESH).wait_recv()
        remap_tracer(lev, t, t, recv, out_ref, pick_s, sum_s, th_s, idx_s, dt_s, rt_s, s_s, q_s, c_s, f_s)
        return 0

    lax.fori_loop(0, NT, settle, 0)

    def drain(t, _):
        for k in range(1, ND):
            across(t, k).wait_send()

        @pl.when(has_south)
        def _():
            for j in range(3):
                to_south(t, j).wait_send()

        @pl.when(has_north)
        def _():
            for j in range(3, 6):
                to_north(t, j).wait_send()
        return 0

    lax.fori_loop(0, NT, drain, 0)

    @pl.when(has_south)
    def _():
        edge_copy().wait_send()


def shards(tracers, courant_lon, courant_lat, level_counts, thick_source, eta_weights):
    dma, any_, vmem = pltpu.SemaphoreType.DMA, pl.BlockSpec(memory_space=pl.ANY), pl.BlockSpec(memory_space=pltpu.VMEM)
    tile9 = pltpu.VMEM((NI + 1, NK, 128), F32)
    return pl.pallas_call(
        functools.partial(kernel, lax.axis_size("lat")),
        name="transport",
        out_shape=jax.ShapeDtypeStruct((NT, NI, NK, SPAN), F32),
        in_specs=[pl.BlockSpec(memory_space=pltpu.SMEM), any_, any_, any_, vmem, vmem],
        out_specs=vmem,
        scratch_shapes=[
            pltpu.VMEM((NT, NS, NI, NX), F32),
            pltpu.VMEM((NT, 6, NS, NX), F32),
            pltpu.VMEM((NT, 4, NS, NX), F32),
            pltpu.VMEM((NS, NI, NX), F32),
            pltpu.VMEM((NS, NI, NX), F32),
            pltpu.VMEM((NS, NX), F32),
            pltpu.VMEM((3, NS, NI, NX), F32),
            pltpu.VMEM((3, NS, NX), F32),
            pltpu.VMEM((3, NS, NI, NX), F32),
            pltpu.VMEM((3, NS, NX), F32),
            pltpu.VMEM((512, 512), jnp.bfloat16),
            pltpu.VMEM((9 * 112, 512), jnp.bfloat16),
            pltpu.VMEM((9 * 112, 512), F32),
            pltpu.VMEM((NT, ND, ROWS, 128), F32),
            pltpu.VMEM((ND, NT, ROWS, 128), F32),
            pltpu.VMEM((NK, 2 * SLOTS), F32),
            pltpu.VMEM((NK + 8, 2 * NK), F32),
            pltpu.VMEM((NK + 8, NX), F32),
            pltpu.VMEM((NK, NX), F32),
            pltpu.VMEM((NI + 1, NK, 128), jnp.int32),
            tile9,
            tile9,
            pltpu.VMEM((2, NK, 128), F32),
            pltpu.VMEM((SLOTS, NX), F32),
            pltpu.VMEM((NK, NX), F32),
            pltpu.VMEM((NK + 8, NX), F32),
            pltpu.VMEM((NK + 8, 128), F32),
            dma((NT,)),
            dma((NT, 4)),
            dma((2,)),
            dma((2,)),
            dma((NT, 6)),
            dma((NT, 6)),
            dma((NT, ND)),
            dma((NT, ND)),
            dma((NT,)),
        ],
        compiler_params=pltpu.CompilerParams(collective_id=0, has_side_effects=True, vmem_limit_bytes=57 << 20),
    )(level_counts, jnp.swapaxes(tracers, 1, 2), jnp.swapaxes(courant_lon, 0, 1), jnp.swapaxes(courant_lat, 0, 1),
      thick_source, eta_weights.reshape(1, NK))


def solution(mesh):
    return jax.shard_map(
        shards,
        mesh=mesh,
        in_specs=(
            P(None, "lat", "lev", None),
            P("lat", "lev", None),
            P("lat", "lev", None),
            P(),
            P("lat", None, "lev"),
            P(),
        ),
        out_specs=P(None, "lat", None, "lev"),
        check_vma=False,
    )
```

```python
import functools
import jax
import jax.numpy as jnp
from jax import lax
from jax.experimental import pallas as pl
from jax.experimental.pallas import tpu as pltpu
from jax.sharding import PartitionSpec as P

MESH = pl.DeviceIdType.MESH
HI = lax.Precision.HIGHEST
F32 = jnp.float32
NT, NI, NS, NX, ND, NK = 8, 8, 13, 1152, 8, 72
SPAN = NX // ND
ROWS = 120
SLOTS = ND * NS
LINES = 4
ORDER = (1, 7, 2, 6, 3, 5, 4)


def gather(v, idx, axis):
    return jnp.take_along_axis(v, idx, axis=axis, mode="promise_in_bounds")


def iota(shape, axis):
    return lax.broadcasted_iota(jnp.int32, shape, axis)


def face_weights(c):
    m = jnp.abs(c)
    r = 1.0 - m
    cm = c * m
    return c * r * r * (1.0 / 12.0), cm * (3.0 - 2.0 * m), cm * r * (-1.0 / 12.0)


def flux_of(w, a, behind, ahead, a_behind, a_ahead):
    up = w[0] >= 0.0
    return w[0] * a + w[1] * jnp.where(up, behind, ahead) + w[2] * jnp.where(up, a_behind, a_ahead)


def face(q2, q1, q, qa):
    return 7.0 * (q1 + q) - (q2 + qa)


def edges(t, rows, inner, wedge, edge_s):
    def column(k, _):
        lanes = pl.ds(pl.multiple_of(k * 128, 128), 128)
        for lo, hi in ((0, 8), (8, NS)):
            n0, n1, n2, s3, s2, s1 = [rows[t, j, lo:hi, lanes] for j in range(6)]
            q0, q5, q6, q7 = [inner[t, j, lo:hi, lanes] for j in range(4)]
            a8 = face(q6, q7, n0, n1)
            edge_s[0, lo:hi, lanes] = face(s3, s2, s1, q0)
            edge_s[1, lo:hi, lanes] = a8
            edge_s[2, lo:hi, lanes] = flux_of(
                [wedge[j, lo:hi, lanes] for j in range(3)], a8, q7, n0, face(q5, q6, q7, n0), face(q7, n0, n1, n2))
        return 0

    lax.fori_loop(0, NX // 128, column, 0)


def stencil():
    p, c = iota((4 * 128, 4 * 128), 0), iota((4 * 128, 4 * 128), 1)
    u, kind = p & 127, c >> 7
    at = jnp.where(p < 256, u, jnp.where(u >= 64, u - 128, u + 128)) - (c & 127)
    near = at + jnp.where(kind == 1, 1, jnp.where(kind == 2, -1, 0))
    value = jnp.where((near == -1) | (near == 0), 7.0, jnp.where((near == -2) | (near == 1), -1.0, 0.0))
    return jnp.where(kind == 3, jnp.where(at == -1, 1.0, 0.0), value).astype(jnp.bfloat16)


def halves(v):
    hi = v.astype(jnp.bfloat16)
    return hi, (v - hi.astype(F32)).astype(jnp.bfloat16)


def lane_stencil(t, xs, sten, taps, faces):
    nk = NX // 128
    pad = jnp.zeros((8, 128), F32)
    lane = iota((NS * NI, 128), 1)
    for k in range(nk):
        col = [xs[t, :, :, 128 * j:128 * j + 128].reshape(NS * NI, 128) for j in ((k + nk - 1) % nk, k, (k + 1) % nk)]
        both = halves(jnp.concatenate([col[1], pad], axis=0)) + halves(
            jnp.concatenate([jnp.where(lane >= 64, col[0], col[2]), pad], axis=0))
        for j, piece in enumerate(both):
            taps[112 * k:112 * k + 112, 128 * j:128 * j + 128] = piece
    faces[...] = jnp.dot(taps[...], sten[...], preferred_element_type=F32)


def horizontal(t, xs, rows, edge_s, wlat, wlon, sten, taps, faces, send):
    sub, lane = iota((8, 128), 0), iota((8, 128), 1)
    first, second, last = sub == 0, sub == 1, sub == 7
    nk = NX // 128
    lane_stencil(t, xs, sten, taps, faces)

    def wide(ref, l, k):
        return jnp.broadcast_to(ref[l:l + 1, 128 * k:128 * k + 128], (8, 128))

    for l in range(NS):
        q = [xs[t, l, :, 128 * k:128 * k + 128] for k in range(nk)]
        flux = []
        for k in range(nk):
            a, a_west, a_east, west = [faces[112 * k + 8 * l:112 * k + 8 * l + 8, 128 * j:128 * j + 128] for j in range(4)]
            flux.append(flux_of([wlon[j, l, :, 128 * k:128 * k + 128] for j in range(3)], a, west, q[k], a_west, a_east))
        turned = [pltpu.roll(f, 127, 1) for f in flux]
        h = []
        for k in range(nk):
            s1 = wide(rows.at[t, 5], l, k)
            q1 = jnp.where(first, s1, pltpu.roll(q[k], 1, 0))
            q2 = jnp.where(first, wide(rows.at[t, 4], l, k), jnp.where(second, s1, pltpu.roll(q[k], 2, 0)))
            qa = jnp.where(last, wide(rows.at[t, 0], l, k), pltpu.roll(q[k], 7, 0))
            b = face(q2, q1, q[k], qa)
            b1 = jnp.where(first, wide(edge_s.at[0], l, k), pltpu.roll(b, 1, 0))
            ba = jnp.where(last, wide(edge_s.at[1], l, k), pltpu.roll(b, 7, 0))
            g = flux_of([wlat[j, l, :, 128 * k:128 * k + 128] for j in range(3)], b, q1, q[k], b1, ba)
            ga = jnp.where(last, wide(edge_s.at[2], l, k), pltpu.roll(g, 7, 0))
            flux_east = jnp.where(lane < 127, turned[k], turned[(k + 1) % nk])
            h.append((q[k] - (flux_east - flux[k])) - (ga - g))
        tail, at = 104 + 8 * (l // 8), 16 * (l % 8)
        for e in range(ND):
            send[t, e, 8 * l:8 * l + 8, :] = jnp.where(lane >= 16 * e, h[e], h[e + 1]) if e else h[0]
            turn = (128 - 16 * e + at) % 128
            piece = pltpu.roll(h[e + 1], turn, 1) if turn else h[e + 1]
            send[t, e, tail:tail + 8, at:at + 16] = piece[:, at:at + 16]


def split(v, parts):
    out = []
    for _ in range(parts):
        p = v.astype(jnp.bfloat16)
        out.append(p)
        v = v - p.astype(F32)
    return jnp.concatenate(out, axis=0)


def zero_one(mask, parts):
    return jnp.concatenate([jnp.where(mask, 1.0, 0.0)] * parts, axis=1)


def mul(m, v):
    return jnp.dot(m.astype(jnp.bfloat16), v, preferred_element_type=F32)


def prep(lev, cnt_ref, thick_ref, eta_ref, pick_s, sum_s, su_s, th_s, idx_s, dt_s, rt_s, fr_s):
    for i in range(NI):
        th_s[:, 128 * i:128 * i + 128] = pltpu.roll(thick_ref[i, :, 0:128], lax.rem(16 * lev, 128), 1)
        th_s[:, NX - 128 + 16 * i:NX - 112 + 16 * i] = thick_ref[i, :, 128:SPAN]
    level, slot = iota((NK, SLOTS), 0), iota((NK, SLOTS), 1)
    source = jnp.zeros((NK, SLOTS), jnp.int32)
    start = jnp.int32(0)
    for d in range(ND):
        c = cnt_ref[d]
        source = jnp.where((level >= start) & (level < start + c), level - start + NS * d, source)
        start = start + c
    pick_s[...] = zero_one(source == slot, 2)
    sum_s[...] = zero_one(iota((NK + 8, NK), 1) < iota((NK + 8, NK), 0), 2)
    r72, l72 = iota((NK, NK), 0), iota((NK, NK), 1)
    eb = jnp.broadcast_to(eta_ref[...], (NK, NK))
    tot = jnp.sum(eb, axis=1, keepdims=True)
    cum = jnp.sum(jnp.where(l72 <= r72, eb, 0.0), axis=1, keepdims=True)
    own = jnp.sum(jnp.where(l72 == r72, eb, 0.0), axis=1, keepdims=True)
    fr_s[0] = jnp.broadcast_to(cum / tot, (NK, 128))
    fr_s[1] = jnp.broadcast_to(own / tot, (NK, 128))
    su_s[...] = mul(zero_one(iota((NK + 8, NK), 1) < iota((NK + 8, NK), 0), 3), split(th_s[...], 3))

    def one(ct, _):
        lanes = pl.ds(pl.multiple_of(ct * 128, 128), 128)
        ps = jnp.broadcast_to(su_s[NK:NK + 1, lanes], (8, 128))
        for tb in range(NK // 8):
            at = slice(8 * tb, 8 * tb + 8)
            t = ps * fr_s[0, at, :]
            rt_s[ct, at, :] = 1.0 / (ps * fr_s[1, at, :])
            n = jnp.zeros((8, 128), jnp.int32)
            for r in range(NK):
                n = jnp.where(jnp.broadcast_to(su_s[r + 1:r + 2, lanes], (8, 128)) <= t, r + 1, n)
            loc, vb = n & 7, n >> 3
            g = ps
            gh = jnp.zeros((8, 128), F32)
            for v in range(NK // 8):
                hit = vb == v
                g = jnp.where(hit, gather(su_s[8 * v:8 * v + 8, lanes], loc, 0), g)
                gh = jnp.where(hit, gather(th_s[8 * v:8 * v + 8, lanes], loc, 0), gh)
            idx_s[ct, at, :] = n
            dt_s[ct, at, :] = jnp.clip(t - g, 0.0, gh)
        return 0

    lax.fori_loop(0, NI + 1, one, 0)


def block_turn(p):
    r, l = iota((8, 128), 0), iota((8, 128), 1)
    p = gather(p, (l + 16 * r) & 127, 1)
    p = gather(p, (r - (l >> 4)) & 7, 0)
    return gather(p, ((16 * r - (l & 112)) & 127) + (l & 15), 1)


def remap_tracer(lev, t, slot, recv, stage, pick_s, sum_s, th_s, idx_s, dt_s, rt_s, s_s, q_s, c_s, f_s):
    for d in range(ND):
        a, b = slice(NS * d, NS * d + 8), slice(NS * d + 8, NS * d + NS)
        for ct in range(NI):
            lanes = slice(128 * ct, 128 * ct + 128)
            s_s[a, lanes] = recv[d, t, pl.ds(ct, 8, stride=8), :]
            s_s[b, lanes] = recv[d, t, pl.ds(64 + ct, NS - 8, stride=8), :]
        s_s[a, NX - 128:] = block_turn(recv[d, t, 104:112, :])
        s_s[b, NX - 128:] = block_turn(recv[d, t, 112:120, :])[:NS - 8]
    q_s[...] = mul(pick_s[...], split(s_s[...], 2))
    c_s[...] = mul(sum_s[...], split(q_s[...] * th_s[...], 2))
    f_s[0:8, :] = jnp.zeros((8, 128), F32)

    def tile(ct):
        lanes = pl.ds(ct * 128, 128) if isinstance(ct, int) else pl.ds(pl.multiple_of(ct * 128, 128), 128)
        total = jnp.broadcast_to(c_s[NK:NK + 1, lanes], (8, 128))
        for tb in range(NK // 8):
            at = slice(8 * tb, 8 * tb + 8)
            n = idx_s[ct, at, :]
            loc, vb = n & 7, n >> 3
            gc = total
            gq = jnp.zeros((8, 128), F32)
            for v in range(NK // 8):
                hit = vb == v
                gc = jnp.where(hit, gather(c_s[8 * v:8 * v + 8, lanes], loc, 0), gc)
                gq = jnp.where(hit, gather(q_s[8 * v:8 * v + 8, lanes], loc, 0), gq)
            f_s[8 + 8 * tb:16 + 8 * tb, :] = gc + dt_s[ct, at, :] * gq
        return (f_s[8:80, :] - f_s[7:79, :]) * rt_s[ct]

    def main(ct, _):
        stage[slot, ct, :, 0:128] = pltpu.roll(tile(ct), lax.rem(128 - 16 * lev, 128), 1)
        return 0

    lax.fori_loop(0, NI, main, 0)
    res = tile(NI)
    for i in range(NI):
        stage[slot, i, :, 128:SPAN] = res[:, 16 * i:16 * i + 16]


def kernel(lat_axis, cnt_ref, x_hbm, clon_hbm, clat_hbm, thick_ref, eta_ref, out_ref,
           xs, rows, inner, clon, clat, cnorth, wlat, wedge, wlon, edge_s, sten, taps, faces, held, send, recv,
           pick_s, sum_s, su_s, th_s, idx_s, dt_s, rt_s, fr_s, s_s, q_s, c_s, f_s,
           x_sem, i_sem, c_sem, esem, hsend, hrecv, held_sem, rest_sem, ssem, rsem, lsem):
    lat, lev = lax.axis_index("lat"), lax.axis_index("lev")
    has_south, has_north = lat > 0, lat < lat_axis - 1

    small = [pltpu.make_async_copy(clat_hbm, clat, c_sem.at[0]), pltpu.make_async_copy(clon_hbm, clon, c_sem.at[1])]
    loads = [pltpu.make_async_copy(x_hbm.at[t], xs.at[t], x_sem.at[t]) for t in range(NT)]
    def inner_load(t, j):
        return pltpu.make_async_copy(x_hbm.at[t, :, (0, 5, 6, 7)[j], :], inner.at[t, j], i_sem.at[t, j])

    small[0].start()
    small[1].start()
    for t in range(NT):
        loads[t].start()
        for j in range(4):
            inner_load(t, j).start()

    def peer(k):
        return lax.rem(lev + k, ND)

    bar = pltpu.get_barrier_semaphore()
    for k in range(1, ND):
        pl.semaphore_signal(bar, inc=1, device_id=(lat, peer(k)), device_id_type=MESH)

    @pl.when(has_south)
    def _():
        pl.semaphore_signal(bar, inc=1, device_id=(lat - 1, lev), device_id_type=MESH)

    @pl.when(has_north)
    def _():
        pl.semaphore_signal(bar, inc=1, device_id=(lat + 1, lev), device_id_type=MESH)

    below, above = lat_axis // 2 - 1, lat_axis // 2
    up_relays = [lat_axis - 2 * i for i in range(1, LINES)]
    down_relays = [2 * i - 1 for i in range(1, LINES)]

    def one_of(places):
        return functools.reduce(jnp.logical_or, [lat == p for p in places])

    def greet(here, places):
        @pl.when(here)
        def _():
            for p in places:
                pl.semaphore_signal(bar, inc=1, device_id=(p, lev), device_id_type=MESH)

    is_up, is_down = one_of(up_relays), one_of(down_relays)
    greet(lat == above, up_relays)
    greet(lat == below, down_relays)
    greet(is_up, [below])
    greet(is_down, [above])
    others = (jnp.where(has_south, 1, 0) + jnp.where(has_north, 1, 0) + jnp.where(is_up, 1, 0) + jnp.where(is_down, 1, 0)
              + jnp.where(lat == above, LINES - 1, 0) + jnp.where(lat == below, LINES - 1, 0))
    pl.semaphore_wait(bar, ND - 1 + others)

    def edge_copy():
        return pltpu.make_async_remote_copy(clat_hbm.at[:, 0, :], cnorth, esem.at[0], esem.at[1],
                                            device_id=(lat - 1, lev), device_id_type=MESH)

    def to_south(t, j):
        return pltpu.make_async_remote_copy(x_hbm.at[t, :, j, :], rows.at[t, j], hsend.at[t, j], hrecv.at[t, j],
                                            device_id=(lat - 1, lev), device_id_type=MESH)

    def to_north(t, j):
        return pltpu.make_async_remote_copy(x_hbm.at[t, :, 2 + j, :], rows.at[t, j], hsend.at[t, j], hrecv.at[t, j],
                                            device_id=(lat + 1, lev), device_id_type=MESH)

    @pl.when(has_south)
    def _():
        edge_copy().start()

    def up_leg(t, j):
        slot = t // LINES
        return pltpu.make_async_remote_copy(x_hbm.at[t, :, 5 + j, :], held.at[slot, j], hsend.at[t, 3 + j], held_sem.at[slot, j],
                                            device_id=(lat_axis - 2 * (t % LINES), lev), device_id_type=MESH)

    def down_leg(t, j):
        slot = t // LINES
        return pltpu.make_async_remote_copy(x_hbm.at[t, :, j, :], held.at[slot, j], hsend.at[t, j], held_sem.at[slot, j],
                                            device_id=(2 * (t % LINES) - 1, lev), device_id_type=MESH)

    def up_rest(t, j):
        return pltpu.make_async_remote_copy(held.at[t // LINES, j], rows.at[t, 3 + j], rest_sem.at[t // LINES, j], hrecv.at[t, 3 + j],
                                            device_id=(above, lev), device_id_type=MESH)

    def down_rest(t, j):
        return pltpu.make_async_remote_copy(held.at[t // LINES, j], rows.at[t, j], rest_sem.at[t // LINES, j], hrecv.at[t, j],
                                            device_id=(below, lev), device_id_type=MESH)

    def relay(t):
        line = lax.rem(t, LINES)

        @pl.when((t < NT) & (line > 0) & (lat == lat_axis - 2 * line))
        def _():
            for j in range(3):
                up_leg(t, j).wait_recv()
                up_rest(t, j).start()

        @pl.when((t < NT) & (line > 0) & (lat == 2 * line - 1))
        def _():
            for j in range(3):
                down_leg(t, j).wait_recv()
                down_rest(t, j).start()

    for t in range(NT):
        straight = t % LINES == 0

        @pl.when(has_south if straight else has_south & (lat != above))
        def _():
            for j in range(3):
                to_south(t, j).start()

        @pl.when(has_north if straight else has_north & (lat != below))
        def _():
            for j in range(3, 6):
                to_north(t, j).start()

        if not straight:
            @pl.when(lat == above)
            def _():
                for j in range(3):
                    down_leg(t, j).start()

            @pl.when(lat == below)
            def _():
                for j in range(3):
                    up_leg(t, j).start()

    @pl.when(lat == 0)
    def _():
        rows[:, 3:6] = jnp.zeros((NT, 3, NS, NX), F32)

    @pl.when(lat == lat_axis - 1)
    def _():
        rows[:, 0:3] = jnp.zeros((NT, 3, NS, NX), F32)
        cnorth[...] = jnp.zeros_like(cnorth)

    sten[...] = stencil()
    small[0].wait()
    small[1].wait()

    def weigh(l, _):
        for k, w in enumerate(face_weights(clat[l])):
            wlat[k, l] = w
        for k, w in enumerate(face_weights(clon[l])):
            wlon[k, l] = w
        return 0

    lax.fori_loop(0, NS, weigh, 0)

    def clear(t, _):
        for e in range(ND):
            send[t, e, 112:120, :] = jnp.zeros((8, 128), F32)
        return 0

    lax.fori_loop(0, NT, clear, 0)

    @pl.when(has_north)
    def _():
        edge_copy().wait_recv()

    for k, w in enumerate(face_weights(cnorth[...])):
        wedge[k] = w

    def across(t, k):
        e = peer(k)
        return pltpu.make_async_remote_copy(send.at[t, e], recv.at[lev, t], ssem.at[t, k], rsem.at[t, lev],
                                            device_id=(lat, e), device_id_type=MESH)

    def own(t):
        return pltpu.make_async_copy(send.at[t, lev], recv.at[lev, t], lsem.at[t])

    def forward(t, _):
        relay(t + 1)
        pltpu.make_async_copy(x_hbm.at[t], xs.at[t], x_sem.at[t]).wait()

        bent = lax.rem(t, LINES) > 0
        from_above, from_below = bent & (lat == below), bent & (lat == above)

        @pl.when(has_north & ~from_above)
        def _():
            for j in range(3):
                to_south(t, j).wait_recv()

        @pl.when(has_south & ~from_below)
        def _():
            for j in range(3, 6):
                to_north(t, j).wait_recv()

        @pl.when(from_above)
        def _():
            for j in range(3):
                down_rest(t, j).wait_recv()

        @pl.when(from_below)
        def _():
            for j in range(3):
                up_rest(t, j).wait_recv()

        for j in range(4):
            inner_load(t, j).wait()
        edges(t, rows, inner, wedge, edge_s)
        horizontal(t, xs, rows, edge_s, wlat, wlon, sten, taps, faces, send)
        for k in ORDER:
            across(t, k).start()
        own(t).start()
        return 0

    lax.fori_loop(0, NT, forward, 0)

    prep(lev, cnt_ref, thick_ref, eta_ref, pick_s, sum_s, su_s, th_s, idx_s, dt_s, rt_s, fr_s)

    def settle(t, _):
        own(t).wait()
        for k in range(1, ND):
            src = peer(k)
            pltpu.make_async_remote_copy(send.at[t, src], recv.at[src, t], ssem.at[t, k], rsem.at[t, src],
                                         device_id=(lat, src), device_id_type=MESH).wait_recv()
        remap_tracer(lev, t, t, recv, out_ref, pick_s, sum_s, th_s, idx_s, dt_s, rt_s, s_s, q_s, c_s, f_s)
        return 0

    lax.fori_loop(0, NT, settle, 0)

    def drain(t, _):
        for k in range(1, ND):
            across(t, k).wait_send()

        @pl.when(has_south)
        def _():
            for j in range(3):
                to_south(t, j).wait_send()

        @pl.when(has_north)
        def _():
            for j in range(3, 6):
                to_north(t, j).wait_send()
        return 0

    lax.fori_loop(0, NT, drain, 0)

    @pl.when(is_up | is_down)
    def _():
        for slot in range(NT // LINES):
            for j in range(3):
                up_rest(slot * LINES, j).wait_send()

    @pl.when(has_south)
    def _():
        edge_copy().wait_send()


def shards(tracers, courant_lon, courant_lat, level_counts, thick_source, eta_weights):
    dma, any_, vmem = pltpu.SemaphoreType.DMA, pl.BlockSpec(memory_space=pl.ANY), pl.BlockSpec(memory_space=pltpu.VMEM)
    tile9 = pltpu.VMEM((NI + 1, NK, 128), F32)
    return pl.pallas_call(
        functools.partial(kernel, lax.axis_size("lat")),
        name="transport",
        out_shape=jax.ShapeDtypeStruct((NT, NI, NK, SPAN), F32),
        in_specs=[pl.BlockSpec(memory_space=pltpu.SMEM), any_, any_, any_, vmem, vmem],
        out_specs=vmem,
        scratch_shapes=[
            pltpu.VMEM((NT, NS, NI, NX), F32),
            pltpu.VMEM((NT, 6, NS, NX), F32),
            pltpu.VMEM((NT, 4, NS, NX), F32),
            pltpu.VMEM((NS, NI, NX), F32),
            pltpu.VMEM((NS, NI, NX), F32),
            pltpu.VMEM((NS, NX), F32),
            pltpu.VMEM((3, NS, NI, NX), F32),
            pltpu.VMEM((3, NS, NX), F32),
            pltpu.VMEM((3, NS, NI, NX), F32),
            pltpu.VMEM((3, NS, NX), F32),
            pltpu.VMEM((512, 512), jnp.bfloat16),
            pltpu.VMEM((9 * 112, 512), jnp.bfloat16),
            pltpu.VMEM((9 * 112, 512), F32),
            pltpu.VMEM((NT // LINES, 3, NS, NX), F32),
            pltpu.VMEM((NT, ND, ROWS, 128), F32),
            pltpu.VMEM((ND, NT, ROWS, 128), F32),
            pltpu.VMEM((NK, 2 * SLOTS), F32),
            pltpu.VMEM((NK + 8, 2 * NK), F32),
            pltpu.VMEM((NK + 8, NX), F32),
            pltpu.VMEM((NK, NX), F32),
            pltpu.VMEM((NI + 1, NK, 128), jnp.int32),
            tile9,
            tile9,
            pltpu.VMEM((2, NK, 128), F32),
            pltpu.VMEM((SLOTS, NX), F32),
            pltpu.VMEM((NK, NX), F32),
            pltpu.VMEM((NK + 8, NX), F32),
            pltpu.VMEM((NK + 8, 128), F32),
            dma((NT,)),
            dma((NT, 4)),
            dma((2,)),
            dma((2,)),
            dma((NT, 6)),
            dma((NT, 6)),
            dma((NT // LINES, 3)),
            dma((NT // LINES, 3)),
            dma((NT, ND)),
            dma((NT, ND)),
            dma((NT,)),
        ],
        compiler_params=pltpu.CompilerParams(collective_id=0, has_side_effects=True, vmem_limit_bytes=57 << 20),
    )(level_counts, jnp.swapaxes(tracers, 1, 2), jnp.swapaxes(courant_lon, 0, 1), jnp.swapaxes(courant_lat, 0, 1),
      thick_source, eta_weights.reshape(1, NK))


def solution(mesh):
    return jax.shard_map(
        shards,
        mesh=mesh,
        in_specs=(
            P(None, "lat", "lev", None),
            P("lat", "lev", None),
            P("lat", "lev", None),
            P(),
            P("lat", None, "lev"),
            P(),
        ),
        out_specs=P(None, "lat", None, "lev"),
        check_vma=False,
    )
```

```python
import functools
import jax
import jax.numpy as jnp
from jax import lax
from jax.experimental import pallas as pl
from jax.experimental.pallas import tpu as pltpu
from jax.sharding import PartitionSpec as P

MESH = pl.DeviceIdType.MESH
HI = lax.Precision.HIGHEST
F32 = jnp.float32
NT, NI, NS, NX, ND, NK = 8, 8, 13, 1152, 8, 72
SPAN = NX // ND
ROWS = 120
SLOTS = ND * NS
LINES = 3
HELD = -(-NT // LINES)
VMEM1, VMEM2 = 57, 57
ORDER = (1, 7, 2, 6, 3, 5, 4)


def gather(v, idx, axis):
    return jnp.take_along_axis(v, idx, axis=axis, mode="promise_in_bounds")


def iota(shape, axis):
    return lax.broadcasted_iota(jnp.int32, shape, axis)


def face_weights(c):
    m = jnp.abs(c)
    r = 1.0 - m
    cm = c * m
    return c * r * r * (1.0 / 12.0), cm * (3.0 - 2.0 * m), cm * r * (-1.0 / 12.0)


def flux_of(w, a, behind, ahead, a_behind, a_ahead):
    up = w[0] >= 0.0
    return w[0] * a + w[1] * jnp.where(up, behind, ahead) + w[2] * jnp.where(up, a_behind, a_ahead)


def face(q2, q1, q, qa):
    return 7.0 * (q1 + q) - (q2 + qa)


def edges(t, rows, xs, wedge, edge_s):
    def column(k, _):
        lanes = pl.ds(pl.multiple_of(k * 128, 128), 128)
        for lo, hi in ((0, 8), (8, NS)):
            n0, n1, n2, s3, s2, s1 = [rows[t, j, lo:hi, lanes] for j in range(6)]
            q0, q5, q6, q7 = [xs[t, lo:hi, j, lanes] for j in (0, 5, 6, 7)]
            a8 = face(q6, q7, n0, n1)
            edge_s[0, lo:hi, lanes] = face(s3, s2, s1, q0)
            edge_s[1, lo:hi, lanes] = a8
            edge_s[2, lo:hi, lanes] = flux_of(
                [wedge[j, lo:hi, lanes] for j in range(3)], a8, q7, n0, face(q5, q6, q7, n0), face(q7, n0, n1, n2))
        return 0

    lax.fori_loop(0, NX // 128, column, 0)


def stencil():
    p, c = iota((4 * 128, 4 * 128), 0), iota((4 * 128, 4 * 128), 1)
    u, kind = p & 127, c >> 7
    at = jnp.where(p < 256, u, jnp.where(u >= 64, u - 128, u + 128)) - (c & 127)
    near = at + jnp.where(kind == 1, 1, jnp.where(kind == 2, -1, 0))
    value = jnp.where((near == -1) | (near == 0), 7.0, jnp.where((near == -2) | (near == 1), -1.0, 0.0))
    return jnp.where(kind == 3, jnp.where(at == -1, 1.0, 0.0), value).astype(jnp.bfloat16)


def halves(v):
    hi = v.astype(jnp.bfloat16)
    return hi, (v - hi.astype(F32)).astype(jnp.bfloat16)


def lane_stencil(t, xs, sten, taps, faces):
    nk = NX // 128
    pad = jnp.zeros((8, 128), F32)
    lane = iota((NS * NI, 128), 1)
    for k in range(nk):
        col = [xs[t, :, :, 128 * j:128 * j + 128].reshape(NS * NI, 128) for j in ((k + nk - 1) % nk, k, (k + 1) % nk)]
        both = halves(jnp.concatenate([col[1], pad], axis=0)) + halves(
            jnp.concatenate([jnp.where(lane >= 64, col[0], col[2]), pad], axis=0))
        for j, piece in enumerate(both):
            taps[112 * k:112 * k + 112, 128 * j:128 * j + 128] = piece
    faces[...] = jnp.dot(taps[...], sten[...], preferred_element_type=F32)


def horizontal(t, xs, rows, edge_s, wlat, wlon, sten, taps, faces, send):
    sub, lane = iota((8, 128), 0), iota((8, 128), 1)
    first, second, last = sub == 0, sub == 1, sub == 7
    nk = NX // 128
    lane_stencil(t, xs, sten, taps, faces)

    def wide(ref, l, k):
        return jnp.broadcast_to(ref[l:l + 1, 128 * k:128 * k + 128], (8, 128))

    for l in range(NS):
        q = [xs[t, l, :, 128 * k:128 * k + 128] for k in range(nk)]
        flux = []
        for k in range(nk):
            a, a_west, a_east, west = [faces[112 * k + 8 * l:112 * k + 8 * l + 8, 128 * j:128 * j + 128] for j in range(4)]
            flux.append(flux_of([wlon[j, l, :, 128 * k:128 * k + 128] for j in range(3)], a, west, q[k], a_west, a_east))
        turned = [pltpu.roll(f, 127, 1) for f in flux]
        h = []
        for k in range(nk):
            s1 = wide(rows.at[t, 5], l, k)
            q1 = jnp.where(first, s1, pltpu.roll(q[k], 1, 0))
            q2 = jnp.where(first, wide(rows.at[t, 4], l, k), jnp.where(second, s1, pltpu.roll(q[k], 2, 0)))
            qa = jnp.where(last, wide(rows.at[t, 0], l, k), pltpu.roll(q[k], 7, 0))
            b = face(q2, q1, q[k], qa)
            b1 = jnp.where(first, wide(edge_s.at[0], l, k), pltpu.roll(b, 1, 0))
            ba = jnp.where(last, wide(edge_s.at[1], l, k), pltpu.roll(b, 7, 0))
            g = flux_of([wlat[j, l, :, 128 * k:128 * k + 128] for j in range(3)], b, q1, q[k], b1, ba)
            ga = jnp.where(last, wide(edge_s.at[2], l, k), pltpu.roll(g, 7, 0))
            flux_east = jnp.where(lane < 127, turned[k], turned[(k + 1) % nk])
            h.append((q[k] - (flux_east - flux[k])) - (ga - g))
        tail, at = 104 + 8 * (l // 8), 16 * (l % 8)
        for e in range(ND):
            send[t, e, 8 * l:8 * l + 8, :] = jnp.where(lane >= 16 * e, h[e], h[e + 1]) if e else h[0]
            turn = (128 - 16 * e + at) % 128
            piece = pltpu.roll(h[e + 1], turn, 1) if turn else h[e + 1]
            send[t, e, tail:tail + 8, at:at + 16] = piece[:, at:at + 16]


def split(v, parts):
    out = []
    for _ in range(parts):
        p = v.astype(jnp.bfloat16)
        out.append(p)
        v = v - p.astype(F32)
    return jnp.concatenate(out, axis=0)


def zero_one(mask, parts):
    return jnp.concatenate([jnp.where(mask, 1.0, 0.0)] * parts, axis=1)


def below_sum():
    return zero_one(iota((NK + 8, NK), 1) < iota((NK + 8, NK), 0), 2)


def mul(m, v):
    return jnp.dot(m.astype(jnp.bfloat16), v, preferred_element_type=F32)


def prep(lev, cnt_ref, thick_ref, eta_ref, pick_s, sum_s, su_s, th_s, idx_s, dt_s, rt_s, fr_s):
    for i in range(NI):
        th_s[:, 128 * i:128 * i + 128] = pltpu.roll(thick_ref[i, :, 0:128], lax.rem(16 * lev, 128), 1)
        th_s[:, NX - 128 + 16 * i:NX - 112 + 16 * i] = thick_ref[i, :, 128:SPAN]
    level, slot = iota((NK, SLOTS), 0), iota((NK, SLOTS), 1)
    source = jnp.zeros((NK, SLOTS), jnp.int32)
    start = jnp.int32(0)
    for d in range(ND):
        c = cnt_ref[d]
        source = jnp.where((level >= start) & (level < start + c), level - start + NS * d, source)
        start = start + c
    pick_s[...] = zero_one(source == slot, 2)
    sum_s[...] = below_sum()
    r72, l72 = iota((NK, NK), 0), iota((NK, NK), 1)
    eb = jnp.broadcast_to(eta_ref[...], (NK, NK))
    tot = jnp.sum(eb, axis=1, keepdims=True)
    cum = jnp.sum(jnp.where(l72 <= r72, eb, 0.0), axis=1, keepdims=True)
    own = jnp.sum(jnp.where(l72 == r72, eb, 0.0), axis=1, keepdims=True)
    fr_s[0] = jnp.broadcast_to(cum / tot, (NK, 128))
    fr_s[1] = jnp.broadcast_to(own / tot, (NK, 128))
    su_s[...] = mul(zero_one(iota((NK + 8, NK), 1) < iota((NK + 8, NK), 0), 3), split(th_s[...], 3))

    def one(ct, _):
        lanes = pl.ds(pl.multiple_of(ct * 128, 128), 128)
        ps = jnp.broadcast_to(su_s[NK:NK + 1, lanes], (8, 128))
        for tb in range(NK // 8):
            at = slice(8 * tb, 8 * tb + 8)
            t = ps * fr_s[0, at, :]
            rt_s[ct, at, :] = 1.0 / (ps * fr_s[1, at, :])
            n = jnp.zeros((8, 128), jnp.int32)
            for r in range(NK):
                n = jnp.where(jnp.broadcast_to(su_s[r + 1:r + 2, lanes], (8, 128)) <= t, r + 1, n)
            loc, vb = n & 7, n >> 3
            g = ps
            gh = jnp.zeros((8, 128), F32)
            for v in range(NK // 8):
                hit = vb == v
                g = jnp.where(hit, gather(su_s[8 * v:8 * v + 8, lanes], loc, 0), g)
                gh = jnp.where(hit, gather(th_s[8 * v:8 * v + 8, lanes], loc, 0), gh)
            idx_s[ct, at, :] = n
            dt_s[ct, at, :] = jnp.clip(t - g, 0.0, gh)
        return 0

    lax.fori_loop(0, NI + 1, one, 0)


def block_turn(p):
    r, l = iota((8, 128), 0), iota((8, 128), 1)
    p = gather(p, (l + 16 * r) & 127, 1)
    p = gather(p, (r - (l >> 4)) & 7, 0)
    return gather(p, ((16 * r - (l & 112)) & 127) + (l & 15), 1)


def remap_tracer(lev, t, slot, recv, stage, pick_s, sum_s, th_s, idx_s, dt_s, rt_s, s_s, q_s, c_s, f_s, beside=None):
    for d in range(ND):
        a, b = slice(NS * d, NS * d + 8), slice(NS * d + 8, NS * d + NS)
        for ct in range(NI):
            lanes = slice(128 * ct, 128 * ct + 128)
            s_s[a, lanes] = recv[d, t, pl.ds(ct, 8, stride=8), :]
            s_s[b, lanes] = recv[d, t, pl.ds(64 + ct, NS - 8, stride=8), :]
        s_s[a, NX - 128:] = block_turn(recv[d, t, 104:112, :])
        s_s[b, NX - 128:] = block_turn(recv[d, t, 112:120, :])[:NS - 8]
    q_s[...] = mul(pick_s[...], split(s_s[...], 2))
    c_s[...] = mul(sum_s[...], split(q_s[...] * th_s[...], 2))
    f_s[0:8, :] = jnp.zeros((8, 128), F32)

    def tile(ct):
        lanes = pl.ds(ct * 128, 128) if isinstance(ct, int) else pl.ds(pl.multiple_of(ct * 128, 128), 128)
        total = jnp.broadcast_to(c_s[NK:NK + 1, lanes], (8, 128))
        for tb in range(NK // 8):
            at = slice(8 * tb, 8 * tb + 8)
            n = idx_s[ct, at, :]
            loc, vb = n & 7, n >> 3
            gc = total
            gq = jnp.zeros((8, 128), F32)
            for v in range(NK // 8):
                hit = vb == v
                gc = jnp.where(hit, gather(c_s[8 * v:8 * v + 8, lanes], loc, 0), gc)
                gq = jnp.where(hit, gather(q_s[8 * v:8 * v + 8, lanes], loc, 0), gq)
            f_s[8 + 8 * tb:16 + 8 * tb, :] = gc + dt_s[ct, at, :] * gq
        return (f_s[8:80, :] - f_s[7:79, :]) * rt_s[ct]

    def main(ct, _):
        if beside is not None:
            beside(ct)
        stage[slot, ct, :, 0:128] = pltpu.roll(tile(ct), lax.rem(128 - 16 * lev, 128), 1)
        return 0

    lax.fori_loop(0, NI, main, 0)
    res = tile(NI)
    for i in range(NI):
        stage[slot, i, :, 128:SPAN] = res[:, 16 * i:16 * i + 16]


def kernel(lat_axis, cnt_ref, x_hbm, clon_hbm, clat_hbm, thick_ref, eta_ref, done, late, pick_o, th_o, idx_o, dt_o, rt_o,
           xs, rows, clon, clat, cnorth, wlat, wedge, wlon, edge_s, sten, taps, faces, held, send, recv,
           pick_s, sum_s, su_s, th_s, idx_s, dt_s, rt_s, fr_s, s_s, q_s, c_s, f_s, stage,
           x_sem, c_sem, esem, hsend, hrecv, held_sem, rest_sem, ssem, rsem, lsem, psem, osem):
    lat, lev = lax.axis_index("lat"), lax.axis_index("lev")
    has_south, has_north = lat > 0, lat < lat_axis - 1

    small = [pltpu.make_async_copy(clat_hbm, clat, c_sem.at[0]), pltpu.make_async_copy(clon_hbm, clon, c_sem.at[1])]
    loads = [pltpu.make_async_copy(x_hbm.at[t], xs.at[t], x_sem.at[t]) for t in range(NT)]
    small[0].start()
    small[1].start()
    loads[0].start()

    def peer(k):
        return lax.rem(lev + k, ND)

    bar = pltpu.get_barrier_semaphore()
    for k in range(1, ND):
        pl.semaphore_signal(bar, inc=1, device_id=(lat, peer(k)), device_id_type=MESH)

    @pl.when(has_south)
    def _():
        pl.semaphore_signal(bar, inc=1, device_id=(lat - 1, lev), device_id_type=MESH)

    @pl.when(has_north)
    def _():
        pl.semaphore_signal(bar, inc=1, device_id=(lat + 1, lev), device_id_type=MESH)

    below, above = lat_axis // 2 - 1, lat_axis // 2
    up_relays = [lat_axis - 2 * i for i in range(1, LINES)]
    down_relays = [2 * i - 1 for i in range(1, LINES)]

    def one_of(places):
        return functools.reduce(jnp.logical_or, [lat == p for p in places])

    def greet(here, places):
        @pl.when(here)
        def _():
            for p in places:
                pl.semaphore_signal(bar, inc=1, device_id=(p, lev), device_id_type=MESH)

    is_up, is_down = one_of(up_relays), one_of(down_relays)
    greet(lat == above, up_relays)
    greet(lat == below, down_relays)
    greet(is_up, [below])
    greet(is_down, [above])
    others = (jnp.where(has_south, 1, 0) + jnp.where(has_north, 1, 0) + jnp.where(is_up, 1, 0) + jnp.where(is_down, 1, 0)
              + jnp.where(lat == above, LINES - 1, 0) + jnp.where(lat == below, LINES - 1, 0))
    pl.semaphore_wait(bar, ND - 1 + others)

    def edge_copy():
        return pltpu.make_async_remote_copy(clat_hbm.at[:, 0, :], cnorth, esem.at[0], esem.at[1],
                                            device_id=(lat - 1, lev), device_id_type=MESH)

    def to_south(t, j):
        return pltpu.make_async_remote_copy(x_hbm.at[t, :, j, :], rows.at[t, j], hsend.at[t, j], hrecv.at[t, j],
                                            device_id=(lat - 1, lev), device_id_type=MESH)

    def to_north(t, j):
        return pltpu.make_async_remote_copy(x_hbm.at[t, :, 2 + j, :], rows.at[t, j], hsend.at[t, j], hrecv.at[t, j],
                                            device_id=(lat + 1, lev), device_id_type=MESH)

    @pl.when(has_south)
    def _():
        edge_copy().start()

    def up_leg(t, j):
        slot = t // LINES
        return pltpu.make_async_remote_copy(x_hbm.at[t, :, 5 + j, :], held.at[slot, j], hsend.at[t, 3 + j], held_sem.at[slot, j],
                                            device_id=(lat_axis - 2 * (t % LINES), lev), device_id_type=MESH)

    def down_leg(t, j):
        slot = t // LINES
        return pltpu.make_async_remote_copy(x_hbm.at[t, :, j, :], held.at[slot, j], hsend.at[t, j], held_sem.at[slot, j],
                                            device_id=(2 * (t % LINES) - 1, lev), device_id_type=MESH)

    def up_rest(t, j):
        return pltpu.make_async_remote_copy(held.at[t // LINES, j], rows.at[t, 3 + j], rest_sem.at[t // LINES, j], hrecv.at[t, 3 + j],
                                            device_id=(above, lev), device_id_type=MESH)

    def down_rest(t, j):
        return pltpu.make_async_remote_copy(held.at[t // LINES, j], rows.at[t, j], rest_sem.at[t // LINES, j], hrecv.at[t, j],
                                            device_id=(below, lev), device_id_type=MESH)

    def relay(t):
        line = lax.rem(t, LINES)

        @pl.when((t < NT) & (line > 0) & (lat == lat_axis - 2 * line))
        def _():
            for j in range(3):
                up_leg(t, j).wait_recv()
                up_rest(t, j).start()

        @pl.when((t < NT) & (line > 0) & (lat == 2 * line - 1))
        def _():
            for j in range(3):
                down_leg(t, j).wait_recv()
                down_rest(t, j).start()

    for t in range(NT):
        straight = t % LINES == 0

        @pl.when(has_south if straight else has_south & (lat != above))
        def _():
            for j in range(3):
                to_south(t, j).start()

        @pl.when(has_north if straight else has_north & (lat != below))
        def _():
            for j in range(3, 6):
                to_north(t, j).start()

        if not straight:
            @pl.when(lat == above)
            def _():
                for j in range(3):
                    down_leg(t, j).start()

            @pl.when(lat == below)
            def _():
                for j in range(3):
                    up_leg(t, j).start()

        if t > 0:
            loads[t].start()

    @pl.when(lat == 0)
    def _():
        rows[:, 3:6] = jnp.zeros((NT, 3, NS, NX), F32)

    @pl.when(lat == lat_axis - 1)
    def _():
        rows[:, 0:3] = jnp.zeros((NT, 3, NS, NX), F32)
        cnorth[...] = jnp.zeros_like(cnorth)

    sten[...] = stencil()
    small[0].wait()
    small[1].wait()

    def weigh(l, _):
        for k, w in enumerate(face_weights(clat[l])):
            wlat[k, l] = w
        for k, w in enumerate(face_weights(clon[l])):
            wlon[k, l] = w
        return 0

    lax.fori_loop(0, NS, weigh, 0)

    def clear(t, _):
        for e in range(ND):
            send[t, e, 112:120, :] = jnp.zeros((8, 128), F32)
        return 0

    lax.fori_loop(0, NT, clear, 0)

    @pl.when(has_north)
    def _():
        edge_copy().wait_recv()

    for k, w in enumerate(face_weights(cnorth[...])):
        wedge[k] = w

    def across(t, k, last=False):
        e = peer(k)
        return pltpu.make_async_remote_copy(send.at[t, e], late.at[lev] if last else recv.at[lev, t], ssem.at[t, k], rsem.at[t, lev],
                                            device_id=(lat, e), device_id_type=MESH)

    def own(t, last=False):
        return pltpu.make_async_copy(send.at[t, lev], late.at[lev] if last else recv.at[lev, t], lsem.at[t])

    def forward(t, _):
        relay(t + 1)
        pltpu.make_async_copy(x_hbm.at[t], xs.at[t], x_sem.at[t]).wait()

        bent = lax.rem(t, LINES) > 0
        from_above, from_below = bent & (lat == below), bent & (lat == above)

        @pl.when(has_north & ~from_above)
        def _():
            for j in range(3):
                to_south(t, j).wait_recv()

        @pl.when(has_south & ~from_below)
        def _():
            for j in range(3, 6):
                to_north(t, j).wait_recv()

        @pl.when(from_above)
        def _():
            for j in range(3):
                down_rest(t, j).wait_recv()

        @pl.when(from_below)
        def _():
            for j in range(3):
                up_rest(t, j).wait_recv()

        edges(t, rows, xs, wedge, edge_s)
        horizontal(t, xs, rows, edge_s, wlat, wlon, sten, taps, faces, send)

        @pl.when(t < NT - 1)
        def _():
            for k in ORDER:
                across(t, k).start()
            own(t).start()

        @pl.when(t == NT - 1)
        def _():
            for k in ORDER:
                across(t, k, True).start()
            own(t, True).start()
        return 0

    lax.fori_loop(0, NT, forward, 0)

    prep(lev, cnt_ref, thick_ref, eta_ref, pick_s, sum_s, su_s, th_s, idx_s, dt_s, rt_s, fr_s)

    kept = [pltpu.make_async_copy(v, o, psem.at[i]) for i, (v, o) in enumerate(
        ((pick_s, pick_o), (th_s, th_o), (idx_s, idx_o), (dt_s, dt_o), (rt_s, rt_o)))]
    for c in kept:
        c.start()

    def put(t, slot):
        return pltpu.make_async_copy(stage.at[slot], done.at[t], osem.at[slot])

    def settle(t, _):
        own(t).wait()
        for k in range(1, ND):
            src = peer(k)
            pltpu.make_async_remote_copy(send.at[t, src], recv.at[src, t], ssem.at[t, k], rsem.at[t, src],
                                         device_id=(lat, src), device_id_type=MESH).wait_recv()
        slot = lax.rem(t, 2)

        @pl.when(t >= 2)
        def _():
            put(t - 2, slot).wait()

        remap_tracer(lev, t, slot, recv, stage, pick_s, sum_s, th_s, idx_s, dt_s, rt_s, s_s, q_s, c_s, f_s)
        put(t, slot).start()
        return 0

    lax.fori_loop(0, NT - 1, settle, 0)
    put(NT - 3, (NT - 3) % 2).wait()
    put(NT - 2, (NT - 2) % 2).wait()
    for c in kept:
        c.wait()
    own(NT - 1, True).wait()
    for k in range(1, ND):
        src = peer(k)
        pltpu.make_async_remote_copy(send.at[NT - 1, src], late.at[src], ssem.at[NT - 1, k], rsem.at[NT - 1, src],
                                     device_id=(lat, src), device_id_type=MESH).wait_recv()

    def drain(t, _):
        for k in range(1, ND):
            across(t, k).wait_send()

        @pl.when(has_south)
        def _():
            for j in range(3):
                to_south(t, j).wait_send()

        @pl.when(has_north)
        def _():
            for j in range(3, 6):
                to_north(t, j).wait_send()
        return 0

    lax.fori_loop(0, NT, drain, 0)

    for t in range(NT):
        line = t % LINES
        if line:
            @pl.when((lat == lat_axis - 2 * line) | (lat == 2 * line - 1))
            def _():
                for j in range(3):
                    up_rest(t, j).wait_send()

    @pl.when(has_south)
    def _():
        edge_copy().wait_send()


def finish(done, late, pick_h, th_h, idx_h, dt_h, rt_h, out, recv, pick_s, sum_s, th_s, idx_s, dt_s, rt_s, s_s, q_s, c_s, f_s, stage,
           isem, csem, osem):
    loads = [pltpu.make_async_copy(h, v, isem.at[i]) for i, (h, v) in enumerate(
        ((late, recv.at[:, 0]), (pick_h, pick_s), (th_h, th_s), (idx_h, idx_s), (dt_h, dt_s), (rt_h, rt_s)))]

    def fetch(t):
        return pltpu.make_async_copy(done.at[t], stage.at[t], csem.at[t])

    def write(t):
        return pltpu.make_async_copy(stage.at[t], out.at[t], osem.at[t])

    def lay_down(t):
        @pl.when(t < NT - 1)
        def _():
            fetch(t).wait()
            write(t).start()

    for c in loads:
        c.start()
    for t in range(NT - 1):
        fetch(t).start()
    sum_s[...] = below_sum()
    for c in loads:
        c.wait()
    remap_tracer(lax.axis_index("lev"), 0, NT - 1, recv, stage, pick_s, sum_s, th_s, idx_s, dt_s, rt_s, s_s, q_s, c_s, f_s, lay_down)
    write(NT - 1).start()
    for t in range(NT):
        write(t).wait()


def shards(tracers, courant_lon, courant_lat, level_counts, thick_source, eta_weights):
    dma, any_, vmem = pltpu.SemaphoreType.DMA, pl.BlockSpec(memory_space=pl.ANY), pl.BlockSpec(memory_space=pltpu.VMEM)
    tile9 = pltpu.VMEM((NI + 1, NK, 128), F32)
    pick = pltpu.VMEM((NK, 2 * SLOTS), F32)
    sums = pltpu.VMEM((NK + 8, 2 * NK), F32)
    thick, places = pltpu.VMEM((NK, NX), F32), pltpu.VMEM((NI + 1, NK, 128), jnp.int32)
    stage = pltpu.VMEM((2, NI, NK, SPAN), F32)

    def shape(v):
        return jax.ShapeDtypeStruct(v.shape, v.dtype)

    parts = pl.pallas_call(
        functools.partial(kernel, lax.axis_size("lat")),
        name="transport",
        out_shape=(jax.ShapeDtypeStruct((NT - 1, NI, NK, SPAN), F32), jax.ShapeDtypeStruct((ND, ROWS, 128), F32),
                   shape(pick), shape(thick), shape(places), shape(tile9), shape(tile9)),
        in_specs=[pl.BlockSpec(memory_space=pltpu.SMEM), any_, any_, any_, vmem, vmem],
        out_specs=(any_,) * 7,
        scratch_shapes=[
            pltpu.VMEM((NT, NS, NI, NX), F32),
            pltpu.VMEM((NT, 6, NS, NX), F32),
            pltpu.VMEM((NS, NI, NX), F32),
            pltpu.VMEM((NS, NI, NX), F32),
            pltpu.VMEM((NS, NX), F32),
            pltpu.VMEM((3, NS, NI, NX), F32),
            pltpu.VMEM((3, NS, NX), F32),
            pltpu.VMEM((3, NS, NI, NX), F32),
            pltpu.VMEM((3, NS, NX), F32),
            pltpu.VMEM((512, 512), jnp.bfloat16),
            pltpu.VMEM((9 * 112, 512), jnp.bfloat16),
            pltpu.VMEM((9 * 112, 512), F32),
            pltpu.VMEM((HELD, 3, NS, NX), F32),
            pltpu.VMEM((NT, ND, ROWS, 128), F32),
            pltpu.VMEM((ND, NT, ROWS, 128), F32),
            pick,
            sums,
            pltpu.VMEM((NK + 8, NX), F32),
            thick,
            places,
            tile9,
            tile9,
            pltpu.VMEM((2, NK, 128), F32),
            pltpu.VMEM((SLOTS, NX), F32),
            pltpu.VMEM((NK, NX), F32),
            pltpu.VMEM((NK + 8, NX), F32),
            pltpu.VMEM((NK + 8, 128), F32),
            stage,
            dma((NT,)),
            dma((2,)),
            dma((2,)),
            dma((NT, 6)),
            dma((NT, 6)),
            dma((HELD, 3)),
            dma((HELD, 3)),
            dma((NT, ND)),
            dma((NT, ND)),
            dma((NT,)),
            dma((5,)),
            dma((2,)),
        ],
        compiler_params=pltpu.CompilerParams(collective_id=0, has_side_effects=True, vmem_limit_bytes=VMEM1 << 20),
    )(level_counts, jnp.swapaxes(tracers, 1, 2), jnp.swapaxes(courant_lon, 0, 1), jnp.swapaxes(courant_lat, 0, 1),
      thick_source, eta_weights.reshape(1, NK))
    return pl.pallas_call(
        finish,
        name="finish",
        out_shape=jax.ShapeDtypeStruct((NT, NI, NK, SPAN), F32),
        in_specs=[any_] * 7,
        out_specs=any_,
        scratch_shapes=[
            pltpu.VMEM((ND, 1, ROWS, 128), F32), pick, sums, thick, places, tile9, tile9,
            pltpu.VMEM((SLOTS, NX), F32), pltpu.VMEM((NK, NX), F32), pltpu.VMEM((NK + 8, NX), F32), pltpu.VMEM((NK + 8, 128), F32),
            pltpu.VMEM((NT, NI, NK, SPAN), F32), dma((6,)), dma((NT - 1,)), dma((NT,)),
        ],
        compiler_params=pltpu.CompilerParams(vmem_limit_bytes=VMEM2 << 20),
    )(*parts)


def solution(mesh):
    return jax.shard_map(
        shards,
        mesh=mesh,
        in_specs=(
            P(None, "lat", "lev", None),
            P("lat", "lev", None),
            P("lat", "lev", None),
            P(),
            P("lat", None, "lev"),
            P(),
        ),
        out_specs=P(None, "lat", None, "lev"),
        check_vma=False,
    )
```

```python
import functools
import jax
import jax.numpy as jnp
from jax import lax
from jax.experimental import pallas as pl
from jax.experimental.pallas import tpu as pltpu
from jax.sharding import PartitionSpec as P

MESH = pl.DeviceIdType.MESH
HI = lax.Precision.HIGHEST
F32 = jnp.float32
NT, NI, NS, NX, ND, NK = 8, 8, 13, 1152, 8, 72
SPAN = NX // ND
ROWS, HEAD = 120, 72
SLOTS = ND * NS
LINES = 3
HELD = -(-NT // LINES)
VMEM1, VMEM2 = 57, 57
ORDER = (1, 7, 2, 6, 3, 5, 4)


def gather(v, idx, axis):
    return jnp.take_along_axis(v, idx, axis=axis, mode="promise_in_bounds")


def iota(shape, axis):
    return lax.broadcasted_iota(jnp.int32, shape, axis)


def face_weights(c):
    m = jnp.abs(c)
    r = 1.0 - m
    cm = c * m
    return c * r * r * (1.0 / 12.0), cm * (3.0 - 2.0 * m), cm * r * (-1.0 / 12.0)


def flux_of(w, a, behind, ahead, a_behind, a_ahead):
    up = w[0] >= 0.0
    return w[0] * a + w[1] * jnp.where(up, behind, ahead) + w[2] * jnp.where(up, a_behind, a_ahead)


def face(q2, q1, q, qa):
    return 7.0 * (q1 + q) - (q2 + qa)


def edges(t, rows, xs, wedge, edge_s):
    def column(k, _):
        lanes = pl.ds(pl.multiple_of(k * 128, 128), 128)
        for lo, hi in ((0, 8), (8, NS)):
            n0, n1, n2, s3, s2, s1 = [rows[t, j, lo:hi, lanes] for j in range(6)]
            q0, q5, q6, q7 = [xs[t, lo:hi, j, lanes] for j in (0, 5, 6, 7)]
            a8 = face(q6, q7, n0, n1)
            edge_s[0, lo:hi, lanes] = face(s3, s2, s1, q0)
            edge_s[1, lo:hi, lanes] = a8
            edge_s[2, lo:hi, lanes] = flux_of(
                [wedge[j, lo:hi, lanes] for j in range(3)], a8, q7, n0, face(q5, q6, q7, n0), face(q7, n0, n1, n2))
        return 0

    lax.fori_loop(0, NX // 128, column, 0)


def stencil():
    p, c = iota((4 * 128, 4 * 128), 0), iota((4 * 128, 4 * 128), 1)
    u, kind = p & 127, c >> 7
    at = jnp.where(p < 256, u, jnp.where(u >= 64, u - 128, u + 128)) - (c & 127)
    near = at + jnp.where(kind == 1, 1, jnp.where(kind == 2, -1, 0))
    value = jnp.where((near == -1) | (near == 0), 7.0, jnp.where((near == -2) | (near == 1), -1.0, 0.0))
    return jnp.where(kind == 3, jnp.where(at == -1, 1.0, 0.0), value).astype(jnp.bfloat16)


def halves(v):
    hi = v.astype(jnp.bfloat16)
    return hi, (v - hi.astype(F32)).astype(jnp.bfloat16)


def lane_stencil(t, xs, sten, taps, faces):
    nk = NX // 128
    pad = jnp.zeros((8, 128), F32)
    lane = iota((NS * NI, 128), 1)
    for k in range(nk):
        col = [xs[t, :, :, 128 * j:128 * j + 128].reshape(NS * NI, 128) for j in ((k + nk - 1) % nk, k, (k + 1) % nk)]
        both = halves(jnp.concatenate([col[1], pad], axis=0)) + halves(
            jnp.concatenate([jnp.where(lane >= 64, col[0], col[2]), pad], axis=0))
        for j, piece in enumerate(both):
            taps[112 * k:112 * k + 112, 128 * j:128 * j + 128] = piece
    faces[...] = jnp.dot(taps[...], sten[...], preferred_element_type=F32)


def longitude(t, xs, wlon, sten, taps, faces, part):
    lane = iota((8, 128), 1)
    nk = NX // 128
    lane_stencil(t, xs, sten, taps, faces)
    for l in range(NS):
        flux = []
        for k in range(nk):
            a, a_west, a_east, west = [faces[112 * k + 8 * l:112 * k + 8 * l + 8, 128 * j:128 * j + 128] for j in range(4)]
            flux.append(flux_of([wlon[j, l, :, 128 * k:128 * k + 128] for j in range(3)], a, west,
                                xs[t, l, :, 128 * k:128 * k + 128], a_west, a_east))
        turned = [pltpu.roll(f, 127, 1) for f in flux]
        for k in range(nk):
            flux_east = jnp.where(lane < 127, turned[k], turned[(k + 1) % nk])
            part[l, :, 128 * k:128 * k + 128] = xs[t, l, :, 128 * k:128 * k + 128] - (flux_east - flux[k])


def latitude(t, levels, xs, rows, edge_s, wlat, part, send):
    sub, lane = iota((8, 128), 0), iota((8, 128), 1)
    first, second, last = sub == 0, sub == 1, sub == 7

    def wide(ref, l, k):
        return jnp.broadcast_to(ref[l:l + 1, 128 * k:128 * k + 128], (8, 128))

    for l in levels:
        h = []
        for k in range(NX // 128):
            q = xs[t, l, :, 128 * k:128 * k + 128]
            s1 = wide(rows.at[t, 5], l, k)
            q1 = jnp.where(first, s1, pltpu.roll(q, 1, 0))
            q2 = jnp.where(first, wide(rows.at[t, 4], l, k), jnp.where(second, s1, pltpu.roll(q, 2, 0)))
            qa = jnp.where(last, wide(rows.at[t, 0], l, k), pltpu.roll(q, 7, 0))
            b = face(q2, q1, q, qa)
            b1 = jnp.where(first, wide(edge_s.at[0], l, k), pltpu.roll(b, 1, 0))
            ba = jnp.where(last, wide(edge_s.at[1], l, k), pltpu.roll(b, 7, 0))
            g = flux_of([wlat[j, l, :, 128 * k:128 * k + 128] for j in range(3)], b, q1, q, b1, ba)
            ga = jnp.where(last, wide(edge_s.at[2], l, k), pltpu.roll(g, 7, 0))
            h.append(part[l, :, 128 * k:128 * k + 128] - (ga - g))
        main, tail, at = 8 * l + (8 if l >= 8 else 0), 112 if l >= 8 else 64, 16 * (l % 8)
        for e in range(ND):
            send[t, e, main:main + 8, :] = jnp.where(lane >= 16 * e, h[e], h[e + 1]) if e else h[0]
            turn = (128 - 16 * e + at) % 128
            piece = pltpu.roll(h[e + 1], turn, 1) if turn else h[e + 1]
            send[t, e, tail:tail + 8, at:at + 16] = piece[:, at:at + 16]


def split(v, parts):
    out = []
    for _ in range(parts):
        p = v.astype(jnp.bfloat16)
        out.append(p)
        v = v - p.astype(F32)
    return jnp.concatenate(out, axis=0)


def zero_one(mask, parts):
    return jnp.concatenate([jnp.where(mask, 1.0, 0.0)] * parts, axis=1)


def below_sum():
    return zero_one(iota((NK + 8, NK), 1) < iota((NK + 8, NK), 0), 2)


def mul(m, v):
    return jnp.dot(m.astype(jnp.bfloat16), v, preferred_element_type=F32)


def prep(lev, cnt_ref, thick_ref, eta_ref, pick_s, sum_s, su_s, th_s, idx_s, dt_s, rt_s, fr_s):
    for i in range(NI):
        th_s[:, 128 * i:128 * i + 128] = pltpu.roll(thick_ref[i, :, 0:128], lax.rem(16 * lev, 128), 1)
        th_s[:, NX - 128 + 16 * i:NX - 112 + 16 * i] = thick_ref[i, :, 128:SPAN]
    level, slot = iota((NK, SLOTS), 0), iota((NK, SLOTS), 1)
    source = jnp.zeros((NK, SLOTS), jnp.int32)
    start = jnp.int32(0)
    for d in range(ND):
        c = cnt_ref[d]
        source = jnp.where((level >= start) & (level < start + c), level - start + NS * d, source)
        start = start + c
    pick_s[...] = zero_one(source == slot, 2)
    sum_s[...] = below_sum()
    r72, l72 = iota((NK, NK), 0), iota((NK, NK), 1)
    eb = jnp.broadcast_to(eta_ref[...], (NK, NK))
    tot = jnp.sum(eb, axis=1, keepdims=True)
    cum = jnp.sum(jnp.where(l72 <= r72, eb, 0.0), axis=1, keepdims=True)
    own = jnp.sum(jnp.where(l72 == r72, eb, 0.0), axis=1, keepdims=True)
    fr_s[0] = jnp.broadcast_to(cum / tot, (NK, 128))
    fr_s[1] = jnp.broadcast_to(own / tot, (NK, 128))
    su_s[...] = mul(zero_one(iota((NK + 8, NK), 1) < iota((NK + 8, NK), 0), 3), split(th_s[...], 3))

    def one(ct, _):
        lanes = pl.ds(pl.multiple_of(ct * 128, 128), 128)
        ps = jnp.broadcast_to(su_s[NK:NK + 1, lanes], (8, 128))
        for tb in range(NK // 8):
            at = slice(8 * tb, 8 * tb + 8)
            t = ps * fr_s[0, at, :]
            rt_s[ct, at, :] = 1.0 / (ps * fr_s[1, at, :])
            n = jnp.zeros((8, 128), jnp.int32)
            for r in range(NK):
                n = jnp.where(jnp.broadcast_to(su_s[r + 1:r + 2, lanes], (8, 128)) <= t, r + 1, n)
            loc, vb = n & 7, n >> 3
            g = ps
            gh = jnp.zeros((8, 128), F32)
            for v in range(NK // 8):
                hit = vb == v
                g = jnp.where(hit, gather(su_s[8 * v:8 * v + 8, lanes], loc, 0), g)
                gh = jnp.where(hit, gather(th_s[8 * v:8 * v + 8, lanes], loc, 0), gh)
            idx_s[ct, at, :] = n
            dt_s[ct, at, :] = jnp.clip(t - g, 0.0, gh)
        return 0

    lax.fori_loop(0, NI + 1, one, 0)


def block_turn(p):
    r, l = iota((8, 128), 0), iota((8, 128), 1)
    p = gather(p, (l + 16 * r) & 127, 1)
    p = gather(p, (r - (l >> 4)) & 7, 0)
    return gather(p, ((16 * r - (l & 112)) & 127) + (l & 15), 1)


def remap_tracer(lev, t, slot, recv, stage, pick_s, sum_s, th_s, idx_s, dt_s, rt_s, s_s, q_s, c_s, f_s, beside=None):
    for d in range(ND):
        a, b = slice(NS * d, NS * d + 8), slice(NS * d + 8, NS * d + NS)
        for ct in range(NI):
            lanes = slice(128 * ct, 128 * ct + 128)
            s_s[a, lanes] = recv[d, t, pl.ds(ct, 8, stride=8), :]
            s_s[b, lanes] = recv[d, t, pl.ds(72 + ct, NS - 8, stride=8), :]
        s_s[a, NX - 128:] = block_turn(recv[d, t, 64:72, :])
        s_s[b, NX - 128:] = block_turn(recv[d, t, 112:120, :])[:NS - 8]
    q_s[...] = mul(pick_s[...], split(s_s[...], 2))
    c_s[...] = mul(sum_s[...], split(q_s[...] * th_s[...], 2))
    f_s[0:8, :] = jnp.zeros((8, 128), F32)

    def tile(ct):
        lanes = pl.ds(ct * 128, 128) if isinstance(ct, int) else pl.ds(pl.multiple_of(ct * 128, 128), 128)
        total = jnp.broadcast_to(c_s[NK:NK + 1, lanes], (8, 128))
        for tb in range(NK // 8):
            at = slice(8 * tb, 8 * tb + 8)
            n = idx_s[ct, at, :]
            loc, vb = n & 7, n >> 3
            gc = total
            gq = jnp.zeros((8, 128), F32)
            for v in range(NK // 8):
                hit = vb == v
                gc = jnp.where(hit, gather(c_s[8 * v:8 * v + 8, lanes], loc, 0), gc)
                gq = jnp.where(hit, gather(q_s[8 * v:8 * v + 8, lanes], loc, 0), gq)
            f_s[8 + 8 * tb:16 + 8 * tb, :] = gc + dt_s[ct, at, :] * gq
        return (f_s[8:80, :] - f_s[7:79, :]) * rt_s[ct]

    def main(ct, _):
        if beside is not None:
            beside(ct)
        stage[slot, ct, :, 0:128] = pltpu.roll(tile(ct), lax.rem(128 - 16 * lev, 128), 1)
        return 0

    lax.fori_loop(0, NI, main, 0)
    res = tile(NI)
    for i in range(NI):
        stage[slot, i, :, 128:SPAN] = res[:, 16 * i:16 * i + 16]


def kernel(lat_axis, cnt_ref, x_hbm, clon_hbm, clat_hbm, thick_ref, eta_ref, done, late, pick_o, th_o, idx_o, dt_o, rt_o,
           xs, rows, clon, clat, cnorth, wlat, wedge, wlon, edge_s, sten, taps, faces, part, held, send, recv,
           pick_s, sum_s, su_s, th_s, idx_s, dt_s, rt_s, fr_s, s_s, q_s, c_s, f_s, stage,
           x_sem, c_sem, esem, hsend, hrecv, held_sem, rest_sem, ssem, rsem, lsem, psem, osem):
    lat, lev = lax.axis_index("lat"), lax.axis_index("lev")
    has_south, has_north = lat > 0, lat < lat_axis - 1

    small = [pltpu.make_async_copy(clat_hbm, clat, c_sem.at[0]), pltpu.make_async_copy(clon_hbm, clon, c_sem.at[1])]
    loads = [pltpu.make_async_copy(x_hbm.at[t], xs.at[t], x_sem.at[t]) for t in range(NT)]
    small[0].start()
    small[1].start()
    loads[0].start()

    def peer(k):
        return lax.rem(lev + k, ND)

    bar = pltpu.get_barrier_semaphore()
    for k in range(1, ND):
        pl.semaphore_signal(bar, inc=1, device_id=(lat, peer(k)), device_id_type=MESH)

    @pl.when(has_south)
    def _():
        pl.semaphore_signal(bar, inc=1, device_id=(lat - 1, lev), device_id_type=MESH)

    @pl.when(has_north)
    def _():
        pl.semaphore_signal(bar, inc=1, device_id=(lat + 1, lev), device_id_type=MESH)

    below, above = lat_axis // 2 - 1, lat_axis // 2
    up_relays = [lat_axis - 2 * i for i in range(1, LINES)]
    down_relays = [2 * i - 1 for i in range(1, LINES)]

    def one_of(places):
        return functools.reduce(jnp.logical_or, [lat == p for p in places])

    def greet(here, places):
        @pl.when(here)
        def _():
            for p in places:
                pl.semaphore_signal(bar, inc=1, device_id=(p, lev), device_id_type=MESH)

    is_up, is_down = one_of(up_relays), one_of(down_relays)
    greet(lat == above, up_relays)
    greet(lat == below, down_relays)
    greet(is_up, [below])
    greet(is_down, [above])
    others = (jnp.where(has_south, 1, 0) + jnp.where(has_north, 1, 0) + jnp.where(is_up, 1, 0) + jnp.where(is_down, 1, 0)
              + jnp.where(lat == above, LINES - 1, 0) + jnp.where(lat == below, LINES - 1, 0))
    pl.semaphore_wait(bar, ND - 1 + others)

    def edge_copy():
        return pltpu.make_async_remote_copy(clat_hbm.at[:, 0, :], cnorth, esem.at[0], esem.at[1],
                                            device_id=(lat - 1, lev), device_id_type=MESH)

    def to_south(t, j):
        return pltpu.make_async_remote_copy(x_hbm.at[t, :, j, :], rows.at[t, j], hsend.at[t, j], hrecv.at[t, j],
                                            device_id=(lat - 1, lev), device_id_type=MESH)

    def to_north(t, j):
        return pltpu.make_async_remote_copy(x_hbm.at[t, :, 2 + j, :], rows.at[t, j], hsend.at[t, j], hrecv.at[t, j],
                                            device_id=(lat + 1, lev), device_id_type=MESH)

    @pl.when(has_south)
    def _():
        edge_copy().start()

    def up_leg(t, j):
        slot = t // LINES
        return pltpu.make_async_remote_copy(x_hbm.at[t, :, 5 + j, :], held.at[slot, j], hsend.at[t, 3 + j], held_sem.at[slot, j],
                                            device_id=(lat_axis - 2 * (t % LINES), lev), device_id_type=MESH)

    def down_leg(t, j):
        slot = t // LINES
        return pltpu.make_async_remote_copy(x_hbm.at[t, :, j, :], held.at[slot, j], hsend.at[t, j], held_sem.at[slot, j],
                                            device_id=(2 * (t % LINES) - 1, lev), device_id_type=MESH)

    def up_rest(t, j):
        return pltpu.make_async_remote_copy(held.at[t // LINES, j], rows.at[t, 3 + j], rest_sem.at[t // LINES, j], hrecv.at[t, 3 + j],
                                            device_id=(above, lev), device_id_type=MESH)

    def down_rest(t, j):
        return pltpu.make_async_remote_copy(held.at[t // LINES, j], rows.at[t, j], rest_sem.at[t // LINES, j], hrecv.at[t, j],
                                            device_id=(below, lev), device_id_type=MESH)

    def relay(t):
        line = lax.rem(t, LINES)

        @pl.when((t < NT) & (line > 0) & (lat == lat_axis - 2 * line))
        def _():
            for j in range(3):
                up_leg(t, j).wait_recv()
                up_rest(t, j).start()

        @pl.when((t < NT) & (line > 0) & (lat == 2 * line - 1))
        def _():
            for j in range(3):
                down_leg(t, j).wait_recv()
                down_rest(t, j).start()

    for t in range(NT):
        straight = t % LINES == 0

        @pl.when(has_south if straight else has_south & (lat != above))
        def _():
            for j in range(3):
                to_south(t, j).start()

        @pl.when(has_north if straight else has_north & (lat != below))
        def _():
            for j in range(3, 6):
                to_north(t, j).start()

        if not straight:
            @pl.when(lat == above)
            def _():
                for j in range(3):
                    down_leg(t, j).start()

            @pl.when(lat == below)
            def _():
                for j in range(3):
                    up_leg(t, j).start()

        if t > 0:
            loads[t].start()

    @pl.when(lat == 0)
    def _():
        rows[:, 3:6] = jnp.zeros((NT, 3, NS, NX), F32)

    @pl.when(lat == lat_axis - 1)
    def _():
        rows[:, 0:3] = jnp.zeros((NT, 3, NS, NX), F32)
        cnorth[...] = jnp.zeros_like(cnorth)

    sten[...] = stencil()
    small[0].wait()
    small[1].wait()

    def weigh(l, _):
        for k, w in enumerate(face_weights(clat[l])):
            wlat[k, l] = w
        for k, w in enumerate(face_weights(clon[l])):
            wlon[k, l] = w
        return 0

    lax.fori_loop(0, NS, weigh, 0)

    def clear(t, _):
        for e in range(ND):
            send[t, e, 112:120, :] = jnp.zeros((8, 128), F32)
        return 0

    lax.fori_loop(0, NT, clear, 0)

    @pl.when(has_north)
    def _():
        edge_copy().wait_recv()

    for k, w in enumerate(face_weights(cnorth[...])):
        wedge[k] = w

    def across(t, k, last=False):
        e = peer(k)
        return pltpu.make_async_remote_copy(send.at[t, e], late.at[lev] if last else recv.at[lev, t], ssem.at[t, k], rsem.at[t, lev],
                                            device_id=(lat, e), device_id_type=MESH)

    def across_part(t, k, lo, hi):
        e = peer(k)
        return pltpu.make_async_remote_copy(send.at[t, e, lo:hi], recv.at[lev, t, lo:hi], ssem.at[t, k], rsem.at[t, lev],
                                            device_id=(lat, e), device_id_type=MESH)

    def own(t, last=False):
        return pltpu.make_async_copy(send.at[t, lev], late.at[lev] if last else recv.at[lev, t], lsem.at[t])

    def forward(t, _):
        pltpu.make_async_copy(x_hbm.at[t], xs.at[t], x_sem.at[t]).wait()
        longitude(t, xs, wlon, sten, taps, faces, part)
        relay(t + 1)

        bent = lax.rem(t, LINES) > 0
        from_above, from_below = bent & (lat == below), bent & (lat == above)

        @pl.when(has_north & ~from_above)
        def _():
            for j in range(3):
                to_south(t, j).wait_recv()

        @pl.when(has_south & ~from_below)
        def _():
            for j in range(3, 6):
                to_north(t, j).wait_recv()

        @pl.when(from_above)
        def _():
            for j in range(3):
                down_rest(t, j).wait_recv()

        @pl.when(from_below)
        def _():
            for j in range(3):
                up_rest(t, j).wait_recv()

        edges(t, rows, xs, wedge, edge_s)
        latitude(t, range(8), xs, rows, edge_s, wlat, part, send)

        @pl.when(t == 0)
        def _():
            for k in ORDER:
                across_part(t, k, 0, HEAD).start()

        latitude(t, range(8, NS), xs, rows, edge_s, wlat, part, send)

        @pl.when(t == 0)
        def _():
            for k in ORDER:
                across_part(t, k, HEAD, ROWS).start()
            own(t).start()

        @pl.when((t > 0) & (t < NT - 1))
        def _():
            for k in ORDER:
                across(t, k).start()
            own(t).start()

        @pl.when(t == NT - 1)
        def _():
            for k in ORDER:
                across(t, k, True).start()
            own(t, True).start()
        return 0

    lax.fori_loop(0, NT, forward, 0)

    prep(lev, cnt_ref, thick_ref, eta_ref, pick_s, sum_s, su_s, th_s, idx_s, dt_s, rt_s, fr_s)

    kept = [pltpu.make_async_copy(v, o, psem.at[i]) for i, (v, o) in enumerate(
        ((pick_s, pick_o), (th_s, th_o), (idx_s, idx_o), (dt_s, dt_o), (rt_s, rt_o)))]
    for c in kept:
        c.start()

    def put(t, slot):
        return pltpu.make_async_copy(stage.at[slot], done.at[t], osem.at[slot])

    def settle(t, _):
        own(t).wait()
        for k in range(1, ND):
            src = peer(k)
            pltpu.make_async_remote_copy(send.at[t, src], recv.at[src, t], ssem.at[t, k], rsem.at[t, src],
                                         device_id=(lat, src), device_id_type=MESH).wait_recv()
        slot = lax.rem(t, 2)

        @pl.when(t >= 2)
        def _():
            put(t - 2, slot).wait()

        remap_tracer(lev, t, slot, recv, stage, pick_s, sum_s, th_s, idx_s, dt_s, rt_s, s_s, q_s, c_s, f_s)
        put(t, slot).start()
        return 0

    lax.fori_loop(0, NT - 1, settle, 0)
    put(NT - 3, (NT - 3) % 2).wait()
    put(NT - 2, (NT - 2) % 2).wait()
    for c in kept:
        c.wait()
    own(NT - 1, True).wait()
    for k in range(1, ND):
        src = peer(k)
        pltpu.make_async_remote_copy(send.at[NT - 1, src], late.at[src], ssem.at[NT - 1, k], rsem.at[NT - 1, src],
                                     device_id=(lat, src), device_id_type=MESH).wait_recv()

    def drain(t, _):
        for k in range(1, ND):
            across(t, k).wait_send()

        @pl.when(has_south)
        def _():
            for j in range(3):
                to_south(t, j).wait_send()

        @pl.when(has_north)
        def _():
            for j in range(3, 6):
                to_north(t, j).wait_send()
        return 0

    lax.fori_loop(0, NT, drain, 0)

    for t in range(NT):
        line = t % LINES
        if line:
            @pl.when((lat == lat_axis - 2 * line) | (lat == 2 * line - 1))
            def _():
                for j in range(3):
                    up_rest(t, j).wait_send()

    @pl.when(has_south)
    def _():
        edge_copy().wait_send()


def finish(done, late, pick_h, th_h, idx_h, dt_h, rt_h, out, recv, pick_s, sum_s, th_s, idx_s, dt_s, rt_s, s_s, q_s, c_s, f_s, stage,
           isem, csem, osem):
    loads = [pltpu.make_async_copy(h, v, isem.at[i]) for i, (h, v) in enumerate(
        ((late, recv.at[:, 0]), (pick_h, pick_s), (th_h, th_s), (idx_h, idx_s), (dt_h, dt_s), (rt_h, rt_s)))]

    def fetch(t):
        return pltpu.make_async_copy(done.at[t], stage.at[t], csem.at[t])

    def write(t):
        return pltpu.make_async_copy(stage.at[t], out.at[t], osem.at[t])

    def lay_down(t):
        @pl.when(t < NT - 1)
        def _():
            fetch(t).wait()
            write(t).start()

    for c in loads:
        c.start()
    for t in range(NT - 1):
        fetch(t).start()
    sum_s[...] = below_sum()
    for c in loads:
        c.wait()
    remap_tracer(lax.axis_index("lev"), 0, NT - 1, recv, stage, pick_s, sum_s, th_s, idx_s, dt_s, rt_s, s_s, q_s, c_s, f_s, lay_down)
    write(NT - 1).start()
    for t in range(NT):
        write(t).wait()


def shards(tracers, courant_lon, courant_lat, level_counts, thick_source, eta_weights):
    dma, any_, vmem = pltpu.SemaphoreType.DMA, pl.BlockSpec(memory_space=pl.ANY), pl.BlockSpec(memory_space=pltpu.VMEM)
    tile9 = pltpu.VMEM((NI + 1, NK, 128), F32)
    pick = pltpu.VMEM((NK, 2 * SLOTS), F32)
    sums = pltpu.VMEM((NK + 8, 2 * NK), F32)
    thick, places = pltpu.VMEM((NK, NX), F32), pltpu.VMEM((NI + 1, NK, 128), jnp.int32)
    stage = pltpu.VMEM((2, NI, NK, SPAN), F32)

    def shape(v):
        return jax.ShapeDtypeStruct(v.shape, v.dtype)

    parts = pl.pallas_call(
        functools.partial(kernel, lax.axis_size("lat")),
        name="transport",
        out_shape=(jax.ShapeDtypeStruct((NT - 1, NI, NK, SPAN), F32), jax.ShapeDtypeStruct((ND, ROWS, 128), F32),
                   shape(pick), shape(thick), shape(places), shape(tile9), shape(tile9)),
        in_specs=[pl.BlockSpec(memory_space=pltpu.SMEM), any_, any_, any_, vmem, vmem],
        out_specs=(any_,) * 7,
        scratch_shapes=[
            pltpu.VMEM((NT, NS, NI, NX), F32),
            pltpu.VMEM((NT, 6, NS, NX), F32),
            pltpu.VMEM((NS, NI, NX), F32),
            pltpu.VMEM((NS, NI, NX), F32),
            pltpu.VMEM((NS, NX), F32),
            pltpu.VMEM((3, NS, NI, NX), F32),
            pltpu.VMEM((3, NS, NX), F32),
            pltpu.VMEM((3, NS, NI, NX), F32),
            pltpu.VMEM((3, NS, NX), F32),
            pltpu.VMEM((512, 512), jnp.bfloat16),
            pltpu.VMEM((9 * 112, 512), jnp.bfloat16),
            pltpu.VMEM((9 * 112, 512), F32),
            pltpu.VMEM((NS, NI, NX), F32),
            pltpu.VMEM((HELD, 3, NS, NX), F32),
            pltpu.VMEM((NT, ND, ROWS, 128), F32),
            pltpu.VMEM((ND, NT, ROWS, 128), F32),
            pick,
            sums,
            pltpu.VMEM((NK + 8, NX), F32),
            thick,
            places,
            tile9,
            tile9,
            pltpu.VMEM((2, NK, 128), F32),
            pltpu.VMEM((SLOTS, NX), F32),
            pltpu.VMEM((NK, NX), F32),
            pltpu.VMEM((NK + 8, NX), F32),
            pltpu.VMEM((NK + 8, 128), F32),
            stage,
            dma((NT,)),
            dma((2,)),
            dma((2,)),
            dma((NT, 6)),
            dma((NT, 6)),
            dma((HELD, 3)),
            dma((HELD, 3)),
            dma((NT, ND)),
            dma((NT, ND)),
            dma((NT,)),
            dma((5,)),
            dma((2,)),
        ],
        compiler_params=pltpu.CompilerParams(collective_id=0, has_side_effects=True, vmem_limit_bytes=VMEM1 << 20),
    )(level_counts, jnp.swapaxes(tracers, 1, 2), jnp.swapaxes(courant_lon, 0, 1), jnp.swapaxes(courant_lat, 0, 1),
      thick_source, eta_weights.reshape(1, NK))
    return pl.pallas_call(
        finish,
        name="finish",
        out_shape=jax.ShapeDtypeStruct((NT, NI, NK, SPAN), F32),
        in_specs=[any_] * 7,
        out_specs=any_,
        scratch_shapes=[
            pltpu.VMEM((ND, 1, ROWS, 128), F32), pick, sums, thick, places, tile9, tile9,
            pltpu.VMEM((SLOTS, NX), F32), pltpu.VMEM((NK, NX), F32), pltpu.VMEM((NK + 8, NX), F32), pltpu.VMEM((NK + 8, 128), F32),
            pltpu.VMEM((NT, NI, NK, SPAN), F32), dma((6,)), dma((NT - 1,)), dma((NT,)),
        ],
        compiler_params=pltpu.CompilerParams(vmem_limit_bytes=VMEM2 << 20),
    )(*parts)


def solution(mesh):
    return jax.shard_map(
        shards,
        mesh=mesh,
        in_specs=(
            P(None, "lat", "lev", None),
            P("lat", "lev", None),
            P("lat", "lev", None),
            P(),
            P("lat", None, "lev"),
            P(),
        ),
        out_specs=P(None, "lat", None, "lev"),
        check_vma=False,
    )
```

```python
import functools
import jax
import jax.numpy as jnp
from jax import lax
from jax.experimental import pallas as pl
from jax.experimental.pallas import tpu as pltpu
from jax.sharding import PartitionSpec as P

MESH = pl.DeviceIdType.MESH
HI = lax.Precision.HIGHEST
F32 = jnp.float32
NT, NI, NS, NX, ND, NK = 8, 8, 13, 1152, 8, 72
SPAN = NX // ND
ROWS, HEAD = 120, 72
SLOTS = ND * NS
LINES = 3
HELD = -(-NT // LINES)
VMEM1, VMEM2 = 57, 57
ORDER = (1, 7, 2, 6, 3, 5, 4)


def gather(v, idx, axis):
    return jnp.take_along_axis(v, idx, axis=axis, mode="promise_in_bounds")


def iota(shape, axis):
    return lax.broadcasted_iota(jnp.int32, shape, axis)


def face_weights(c):
    m = jnp.abs(c)
    r = 1.0 - m
    cm = c * m
    return c * r * r * (1.0 / 12.0), cm * (3.0 - 2.0 * m), cm * r * (-1.0 / 12.0)


def flux_of(w, a, behind, ahead, a_behind, a_ahead):
    up = w[0] >= 0.0
    return w[0] * a + w[1] * jnp.where(up, behind, ahead) + w[2] * jnp.where(up, a_behind, a_ahead)


def face(q2, q1, q, qa):
    return 7.0 * (q1 + q) - (q2 + qa)


def edges(t, rows, xs, wedge, edge_s):
    def column(k, _):
        lanes = pl.ds(pl.multiple_of(k * 128, 128), 128)
        for lo, hi in ((0, 8), (8, NS)):
            n0, n1, n2, s3, s2, s1 = [rows[t, j, lo:hi, lanes] for j in range(6)]
            q0, q5, q6, q7 = [xs[t, lo:hi, j, lanes] for j in (0, 5, 6, 7)]
            a8 = face(q6, q7, n0, n1)
            edge_s[0, lo:hi, lanes] = face(s3, s2, s1, q0)
            edge_s[1, lo:hi, lanes] = a8
            edge_s[2, lo:hi, lanes] = flux_of(
                [wedge[j, lo:hi, lanes] for j in range(3)], a8, q7, n0, face(q5, q6, q7, n0), face(q7, n0, n1, n2))
        return 0

    lax.fori_loop(0, NX // 128, column, 0)


def stencil():
    p, c = iota((4 * 128, 4 * 128), 0), iota((4 * 128, 4 * 128), 1)
    u, kind = p & 127, c >> 7
    at = jnp.where(p < 256, u, jnp.where(u >= 64, u - 128, u + 128)) - (c & 127)
    near = at + jnp.where(kind == 1, 1, jnp.where(kind == 2, -1, 0))
    value = jnp.where((near == -1) | (near == 0), 7.0, jnp.where((near == -2) | (near == 1), -1.0, 0.0))
    return jnp.where(kind == 3, jnp.where(at == -1, 1.0, 0.0), value).astype(jnp.bfloat16)


def halves(v):
    hi = v.astype(jnp.bfloat16)
    return hi, (v - hi.astype(F32)).astype(jnp.bfloat16)


def lane_stencil(t, xs, sten, taps, faces):
    nk = NX // 128
    pad = jnp.zeros((8, 128), F32)
    lane = iota((NS * NI, 128), 1)
    for k in range(nk):
        col = [xs[t, :, :, 128 * j:128 * j + 128].reshape(NS * NI, 128) for j in ((k + nk - 1) % nk, k, (k + 1) % nk)]
        both = halves(jnp.concatenate([col[1], pad], axis=0)) + halves(
            jnp.concatenate([jnp.where(lane >= 64, col[0], col[2]), pad], axis=0))
        for j, piece in enumerate(both):
            taps[112 * k:112 * k + 112, 128 * j:128 * j + 128] = piece
    faces[...] = jnp.dot(taps[...], sten[...], preferred_element_type=F32)


def longitude(t, xs, wlon, sten, taps, faces, part):
    lane = iota((8, 128), 1)
    nk = NX // 128
    lane_stencil(t, xs, sten, taps, faces)
    for l in range(NS):
        flux = []
        for k in range(nk):
            a, a_west, a_east, west = [faces[112 * k + 8 * l:112 * k + 8 * l + 8, 128 * j:128 * j + 128] for j in range(4)]
            flux.append(flux_of([wlon[j, l, :, 128 * k:128 * k + 128] for j in range(3)], a, west,
                                xs[t, l, :, 128 * k:128 * k + 128], a_west, a_east))
        turned = [pltpu.roll(f, 127, 1) for f in flux]
        for k in range(nk):
            flux_east = jnp.where(lane < 127, turned[k], turned[(k + 1) % nk])
            part[l, :, 128 * k:128 * k + 128] = xs[t, l, :, 128 * k:128 * k + 128] - (flux_east - flux[k])


def latitude(t, levels, xs, rows, edge_s, wlat, part, send):
    sub, lane = iota((8, 128), 0), iota((8, 128), 1)
    first, second, last = sub == 0, sub == 1, sub == 7

    def wide(ref, l, k):
        return jnp.broadcast_to(ref[l:l + 1, 128 * k:128 * k + 128], (8, 128))

    for l in levels:
        h = []
        for k in range(NX // 128):
            q = xs[t, l, :, 128 * k:128 * k + 128]
            s1 = wide(rows.at[t, 5], l, k)
            q1 = jnp.where(first, s1, pltpu.roll(q, 1, 0))
            q2 = jnp.where(first, wide(rows.at[t, 4], l, k), jnp.where(second, s1, pltpu.roll(q, 2, 0)))
            qa = jnp.where(last, wide(rows.at[t, 0], l, k), pltpu.roll(q, 7, 0))
            b = face(q2, q1, q, qa)
            b1 = jnp.where(first, wide(edge_s.at[0], l, k), pltpu.roll(b, 1, 0))
            ba = jnp.where(last, wide(edge_s.at[1], l, k), pltpu.roll(b, 7, 0))
            g = flux_of([wlat[j, l, :, 128 * k:128 * k + 128] for j in range(3)], b, q1, q, b1, ba)
            ga = jnp.where(last, wide(edge_s.at[2], l, k), pltpu.roll(g, 7, 0))
            h.append(part[l, :, 128 * k:128 * k + 128] - (ga - g))
        main, tail, at = 8 * l + (8 if l >= 8 else 0), 112 if l >= 8 else 64, 16 * (l % 8)
        for e in range(ND):
            send[t, e, main:main + 8, :] = jnp.where(lane >= 16 * e, h[e], h[e + 1]) if e else h[0]
            turn = (128 - 16 * e + at) % 128
            piece = pltpu.roll(h[e + 1], turn, 1) if turn else h[e + 1]
            send[t, e, tail:tail + 8, at:at + 16] = piece[:, at:at + 16]


def split(v, parts):
    out = []
    for _ in range(parts):
        p = v.astype(jnp.bfloat16)
        out.append(p)
        v = v - p.astype(F32)
    return jnp.concatenate(out, axis=0)


def zero_one(mask, parts):
    return jnp.concatenate([jnp.where(mask, 1.0, 0.0)] * parts, axis=1)


def below_sum():
    return zero_one(iota((NK + 8, NK), 1) < iota((NK + 8, NK), 0), 2)


def mul(m, v):
    return jnp.dot(m.astype(jnp.bfloat16), v, preferred_element_type=F32)


def prep(lev, cnt_ref, thick_ref, eta_ref, pick_s, sum_s, su_s, th_s, idx_s, dt_s, rt_s, fr_s):
    for i in range(NI):
        th_s[:, 128 * i:128 * i + 128] = pltpu.roll(thick_ref[i, :, 0:128], lax.rem(16 * lev, 128), 1)
        th_s[:, NX - 128 + 16 * i:NX - 112 + 16 * i] = thick_ref[i, :, 128:SPAN]
    level, slot = iota((NK, SLOTS), 0), iota((NK, SLOTS), 1)
    source = jnp.zeros((NK, SLOTS), jnp.int32)
    start = jnp.int32(0)
    for d in range(ND):
        c = cnt_ref[d]
        source = jnp.where((level >= start) & (level < start + c), level - start + NS * d, source)
        start = start + c
    pick_s[...] = zero_one(source == slot, 2)
    sum_s[...] = below_sum()
    r72, l72 = iota((NK, NK), 0), iota((NK, NK), 1)
    eb = jnp.broadcast_to(eta_ref[...], (NK, NK))
    tot = jnp.sum(eb, axis=1, keepdims=True)
    cum = jnp.sum(jnp.where(l72 <= r72, eb, 0.0), axis=1, keepdims=True)
    own = jnp.sum(jnp.where(l72 == r72, eb, 0.0), axis=1, keepdims=True)
    fr_s[0] = jnp.broadcast_to(cum / tot, (NK, 128))
    fr_s[1] = jnp.broadcast_to(own / tot, (NK, 128))
    su_s[...] = mul(zero_one(iota((NK + 8, NK), 1) < iota((NK + 8, NK), 0), 3), split(th_s[...], 3))

    def one(ct, _):
        lanes = pl.ds(pl.multiple_of(ct * 128, 128), 128)
        ps = jnp.broadcast_to(su_s[NK:NK + 1, lanes], (8, 128))
        for tb in range(NK // 8):
            at = slice(8 * tb, 8 * tb + 8)
            t = ps * fr_s[0, at, :]
            rt_s[ct, at, :] = 1.0 / (ps * fr_s[1, at, :])
            n = jnp.zeros((8, 128), jnp.int32)
            for r in range(NK):
                n = jnp.where(jnp.broadcast_to(su_s[r + 1:r + 2, lanes], (8, 128)) <= t, r + 1, n)
            loc, vb = n & 7, n >> 3
            g = ps
            gh = jnp.zeros((8, 128), F32)
            for v in range(NK // 8):
                hit = vb == v
                g = jnp.where(hit, gather(su_s[8 * v:8 * v + 8, lanes], loc, 0), g)
                gh = jnp.where(hit, gather(th_s[8 * v:8 * v + 8, lanes], loc, 0), gh)
            idx_s[ct, at, :] = n
            dt_s[ct, at, :] = jnp.clip(t - g, 0.0, gh)
        return 0

    lax.fori_loop(0, NI + 1, one, 0)


def block_turn(p):
    r, l = iota((8, 128), 0), iota((8, 128), 1)
    p = gather(p, (l + 16 * r) & 127, 1)
    p = gather(p, (r - (l >> 4)) & 7, 0)
    return gather(p, ((16 * r - (l & 112)) & 127) + (l & 15), 1)


def remap_tracer(lev, t, slot, recv, stage, pick_s, sum_s, th_s, idx_s, dt_s, rt_s, s_s, q_s, c_s, f_s, ready=None, before=None, after=None):
    for d in range(ND):
        a, b = slice(NS * d, NS * d + 8), slice(NS * d + 8, NS * d + NS)
        for ct in range(NI):
            lanes = slice(128 * ct, 128 * ct + 128)
            s_s[a, lanes] = recv[d, t, pl.ds(ct, 8, stride=8), :]
            s_s[b, lanes] = recv[d, t, pl.ds(72 + ct, NS - 8, stride=8), :]
        s_s[a, NX - 128:] = block_turn(recv[d, t, 64:72, :])
        s_s[b, NX - 128:] = block_turn(recv[d, t, 112:120, :])[:NS - 8]
    q_s[...] = mul(pick_s[...], split(s_s[...], 2))
    c_s[...] = mul(sum_s[...], split(q_s[...] * th_s[...], 2))
    f_s[0:8, :] = jnp.zeros((8, 128), F32)
    if ready is not None:
        ready()

    def tile(ct):
        lanes = pl.ds(ct * 128, 128) if isinstance(ct, int) else pl.ds(pl.multiple_of(ct * 128, 128), 128)
        total = jnp.broadcast_to(c_s[NK:NK + 1, lanes], (8, 128))
        for tb in range(NK // 8):
            at = slice(8 * tb, 8 * tb + 8)
            n = idx_s[ct, at, :]
            loc, vb = n & 7, n >> 3
            gc = total
            gq = jnp.zeros((8, 128), F32)
            for v in range(NK // 8):
                hit = vb == v
                gc = jnp.where(hit, gather(c_s[8 * v:8 * v + 8, lanes], loc, 0), gc)
                gq = jnp.where(hit, gather(q_s[8 * v:8 * v + 8, lanes], loc, 0), gq)
            f_s[8 + 8 * tb:16 + 8 * tb, :] = gc + dt_s[ct, at, :] * gq
        return (f_s[8:80, :] - f_s[7:79, :]) * rt_s[ct]

    res = tile(NI)
    for i in range(NI):
        stage[slot, i, :, 128:SPAN] = res[:, 16 * i:16 * i + 16]

    def main(ct, _):
        if before is not None:
            before(ct)
        stage[slot, ct, :, 0:128] = pltpu.roll(tile(ct), lax.rem(128 - 16 * lev, 128), 1)
        if after is not None:
            after(ct)
        return 0

    lax.fori_loop(0, NI, main, 0)


def kernel(lat_axis, cnt_ref, x_hbm, clon_hbm, clat_hbm, thick_ref, eta_ref, done, late, pick_o, th_o, idx_o, dt_o, rt_o,
           xs, rows, clon, clat, cnorth, wlat, wedge, wlon, edge_s, sten, taps, faces, part, held, send, recv,
           pick_s, sum_s, su_s, th_s, idx_s, dt_s, rt_s, fr_s, s_s, q_s, c_s, f_s, stage,
           x_sem, c_sem, esem, hsend, hrecv, held_sem, rest_sem, ssem, rsem, lsem, psem, osem):
    lat, lev = lax.axis_index("lat"), lax.axis_index("lev")
    has_south, has_north = lat > 0, lat < lat_axis - 1

    small = [pltpu.make_async_copy(clat_hbm, clat, c_sem.at[0]), pltpu.make_async_copy(clon_hbm, clon, c_sem.at[1])]
    loads = [pltpu.make_async_copy(x_hbm.at[t], xs.at[t], x_sem.at[t]) for t in range(NT)]
    small[0].start()
    small[1].start()
    loads[0].start()

    def peer(k):
        return lax.rem(lev + k, ND)

    bar = pltpu.get_barrier_semaphore()
    for k in range(1, ND):
        pl.semaphore_signal(bar, inc=1, device_id=(lat, peer(k)), device_id_type=MESH)

    @pl.when(has_south)
    def _():
        pl.semaphore_signal(bar, inc=1, device_id=(lat - 1, lev), device_id_type=MESH)

    @pl.when(has_north)
    def _():
        pl.semaphore_signal(bar, inc=1, device_id=(lat + 1, lev), device_id_type=MESH)

    below, above = lat_axis // 2 - 1, lat_axis // 2
    up_relays = [lat_axis - 2 * i for i in range(1, LINES)]
    down_relays = [2 * i - 1 for i in range(1, LINES)]

    def one_of(places):
        return functools.reduce(jnp.logical_or, [lat == p for p in places])

    def greet(here, places):
        @pl.when(here)
        def _():
            for p in places:
                pl.semaphore_signal(bar, inc=1, device_id=(p, lev), device_id_type=MESH)

    is_up, is_down = one_of(up_relays), one_of(down_relays)
    greet(lat == above, up_relays)
    greet(lat == below, down_relays)
    greet(is_up, [below])
    greet(is_down, [above])
    others = (jnp.where(has_south, 1, 0) + jnp.where(has_north, 1, 0) + jnp.where(is_up, 1, 0) + jnp.where(is_down, 1, 0)
              + jnp.where(lat == above, LINES - 1, 0) + jnp.where(lat == below, LINES - 1, 0))
    pl.semaphore_wait(bar, ND - 1 + others)

    def edge_copy():
        return pltpu.make_async_remote_copy(clat_hbm.at[:, 0, :], cnorth, esem.at[0], esem.at[1],
                                            device_id=(lat - 1, lev), device_id_type=MESH)

    def to_south(t, j):
        return pltpu.make_async_remote_copy(x_hbm.at[t, :, j, :], rows.at[t, j], hsend.at[t, j], hrecv.at[t, j],
                                            device_id=(lat - 1, lev), device_id_type=MESH)

    def to_north(t, j):
        return pltpu.make_async_remote_copy(x_hbm.at[t, :, 2 + j, :], rows.at[t, j], hsend.at[t, j], hrecv.at[t, j],
                                            device_id=(lat + 1, lev), device_id_type=MESH)

    @pl.when(has_south)
    def _():
        edge_copy().start()

    def up_leg(t, j):
        slot = t // LINES
        return pltpu.make_async_remote_copy(x_hbm.at[t, :, 5 + j, :], held.at[slot, j], hsend.at[t, 3 + j], held_sem.at[slot, j],
                                            device_id=(lat_axis - 2 * (t % LINES), lev), device_id_type=MESH)

    def down_leg(t, j):
        slot = t // LINES
        return pltpu.make_async_remote_copy(x_hbm.at[t, :, j, :], held.at[slot, j], hsend.at[t, j], held_sem.at[slot, j],
                                            device_id=(2 * (t % LINES) - 1, lev), device_id_type=MESH)

    def up_rest(t, j):
        return pltpu.make_async_remote_copy(held.at[t // LINES, j], rows.at[t, 3 + j], rest_sem.at[t // LINES, j], hrecv.at[t, 3 + j],
                                            device_id=(above, lev), device_id_type=MESH)

    def down_rest(t, j):
        return pltpu.make_async_remote_copy(held.at[t // LINES, j], rows.at[t, j], rest_sem.at[t // LINES, j], hrecv.at[t, j],
                                            device_id=(below, lev), device_id_type=MESH)

    def relay(t):
        line = lax.rem(t, LINES)

        @pl.when((t < NT) & (line > 0) & (lat == lat_axis - 2 * line))
        def _():
            for j in range(3):
                up_leg(t, j).wait_recv()
                up_rest(t, j).start()

        @pl.when((t < NT) & (line > 0) & (lat == 2 * line - 1))
        def _():
            for j in range(3):
                down_leg(t, j).wait_recv()
                down_rest(t, j).start()

    for t in range(NT):
        straight = t % LINES == 0

        @pl.when(has_south if straight else has_south & (lat != above))
        def _():
            for j in range(3):
                to_south(t, j).start()

        @pl.when(has_north if straight else has_north & (lat != below))
        def _():
            for j in range(3, 6):
                to_north(t, j).start()

        if not straight:
            @pl.when(lat == above)
            def _():
                for j in range(3):
                    down_leg(t, j).start()

            @pl.when(lat == below)
            def _():
                for j in range(3):
                    up_leg(t, j).start()

        if t > 0:
            loads[t].start()

    @pl.when(lat == 0)
    def _():
        rows[:, 3:6] = jnp.zeros((NT, 3, NS, NX), F32)

    @pl.when(lat == lat_axis - 1)
    def _():
        rows[:, 0:3] = jnp.zeros((NT, 3, NS, NX), F32)
        cnorth[...] = jnp.zeros_like(cnorth)

    sten[...] = stencil()
    small[0].wait()
    small[1].wait()

    def weigh(l, _):
        for k, w in enumerate(face_weights(clat[l])):
            wlat[k, l] = w
        for k, w in enumerate(face_weights(clon[l])):
            wlon[k, l] = w
        return 0

    lax.fori_loop(0, NS, weigh, 0)

    def clear(t, _):
        for e in range(ND):
            send[t, e, 112:120, :] = jnp.zeros((8, 128), F32)
        return 0

    lax.fori_loop(0, NT, clear, 0)

    @pl.when(has_north)
    def _():
        edge_copy().wait_recv()

    for k, w in enumerate(face_weights(cnorth[...])):
        wedge[k] = w

    def across(t, k, last=False):
        e = peer(k)
        return pltpu.make_async_remote_copy(send.at[t, e], late.at[lev] if last else recv.at[lev, t], ssem.at[t, k], rsem.at[t, lev],
                                            device_id=(lat, e), device_id_type=MESH)

    def across_part(t, k, lo, hi):
        e = peer(k)
        return pltpu.make_async_remote_copy(send.at[t, e, lo:hi], recv.at[lev, t, lo:hi], ssem.at[t, k], rsem.at[t, lev],
                                            device_id=(lat, e), device_id_type=MESH)

    def own(t, last=False):
        return pltpu.make_async_copy(send.at[t, lev], late.at[lev] if last else recv.at[lev, t], lsem.at[t])

    def forward(t, _):
        pltpu.make_async_copy(x_hbm.at[t], xs.at[t], x_sem.at[t]).wait()
        longitude(t, xs, wlon, sten, taps, faces, part)
        relay(t + 1)

        bent = lax.rem(t, LINES) > 0
        from_above, from_below = bent & (lat == below), bent & (lat == above)

        @pl.when(has_north & ~from_above)
        def _():
            for j in range(3):
                to_south(t, j).wait_recv()

        @pl.when(has_south & ~from_below)
        def _():
            for j in range(3, 6):
                to_north(t, j).wait_recv()

        @pl.when(from_above)
        def _():
            for j in range(3):
                down_rest(t, j).wait_recv()

        @pl.when(from_below)
        def _():
            for j in range(3):
                up_rest(t, j).wait_recv()

        edges(t, rows, xs, wedge, edge_s)
        latitude(t, range(8), xs, rows, edge_s, wlat, part, send)

        @pl.when(t == 0)
        def _():
            for k in ORDER:
                across_part(t, k, 0, HEAD).start()

        latitude(t, range(8, NS), xs, rows, edge_s, wlat, part, send)

        @pl.when(t == 0)
        def _():
            for k in ORDER:
                across_part(t, k, HEAD, ROWS).start()
            own(t).start()

        @pl.when((t > 0) & (t < NT - 1))
        def _():
            for k in ORDER:
                across(t, k).start()
            own(t).start()

        @pl.when(t == NT - 1)
        def _():
            for k in ORDER:
                across(t, k, True).start()
            own(t, True).start()
        return 0

    lax.fori_loop(0, NT, forward, 0)

    prep(lev, cnt_ref, thick_ref, eta_ref, pick_s, sum_s, su_s, th_s, idx_s, dt_s, rt_s, fr_s)

    kept = [pltpu.make_async_copy(v, o, psem.at[i]) for i, (v, o) in enumerate(
        ((pick_s, pick_o), (th_s, th_o), (idx_s, idx_o), (dt_s, dt_o), (rt_s, rt_o)))]
    for c in kept:
        c.start()

    def put(t, slot):
        return pltpu.make_async_copy(stage.at[slot], done.at[t], osem.at[slot])

    def settle(t, _):
        own(t).wait()
        for k in range(1, ND):
            src = peer(k)
            pltpu.make_async_remote_copy(send.at[t, src], recv.at[src, t], ssem.at[t, k], rsem.at[t, src],
                                         device_id=(lat, src), device_id_type=MESH).wait_recv()
        slot = lax.rem(t, 2)

        @pl.when(t >= 2)
        def _():
            put(t - 2, slot).wait()

        remap_tracer(lev, t, slot, recv, stage, pick_s, sum_s, th_s, idx_s, dt_s, rt_s, s_s, q_s, c_s, f_s)
        put(t, slot).start()
        return 0

    lax.fori_loop(0, NT - 1, settle, 0)
    put(NT - 3, (NT - 3) % 2).wait()
    put(NT - 2, (NT - 2) % 2).wait()
    for c in kept:
        c.wait()
    own(NT - 1, True).wait()
    for k in range(1, ND):
        src = peer(k)
        pltpu.make_async_remote_copy(send.at[NT - 1, src], late.at[src], ssem.at[NT - 1, k], rsem.at[NT - 1, src],
                                     device_id=(lat, src), device_id_type=MESH).wait_recv()

    def drain(t, _):
        for k in range(1, ND):
            across(t, k).wait_send()

        @pl.when(has_south)
        def _():
            for j in range(3):
                to_south(t, j).wait_send()

        @pl.when(has_north)
        def _():
            for j in range(3, 6):
                to_north(t, j).wait_send()
        return 0

    lax.fori_loop(0, NT, drain, 0)

    for t in range(NT):
        line = t % LINES
        if line:
            @pl.when((lat == lat_axis - 2 * line) | (lat == 2 * line - 1))
            def _():
                for j in range(3):
                    up_rest(t, j).wait_send()

    @pl.when(has_south)
    def _():
        edge_copy().wait_send()


def finish(done, late, pick_h, th_h, idx_h, dt_h, rt_h, out, recv, pick_s, sum_s, th_s, idx_s, dt_s, rt_s, s_s, q_s, c_s, f_s, stage,
           isem, csem, osem, wsem):
    loads = [pltpu.make_async_copy(h, v, isem.at[i]) for i, (h, v) in enumerate(
        ((late, recv.at[:, 0]), (pick_h, pick_s), (th_h, th_s), (idx_h, idx_s), (dt_h, dt_s), (rt_h, rt_s)))]

    def fetch(t):
        return pltpu.make_async_copy(done.at[t], stage.at[t], csem.at[t])

    def write(t):
        return pltpu.make_async_copy(stage.at[t], out.at[t], osem.at[t])

    def lay_down(t):
        @pl.when(t < NT - 1)
        def _():
            fetch(t).wait()
            write(t).start()

    def write_row(i):
        return pltpu.make_async_copy(stage.at[NT - 1, i], out.at[NT - 1, i], wsem.at[i])

    def ready():
        for c in loads[3:]:
            c.wait()

    for c in loads:
        c.start()
    for t in range(NT - 1):
        fetch(t).start()
    sum_s[...] = below_sum()
    for c in loads[:3]:
        c.wait()
    remap_tracer(lax.axis_index("lev"), 0, NT - 1, recv, stage, pick_s, sum_s, th_s, idx_s, dt_s, rt_s, s_s, q_s, c_s, f_s,
                 ready, lay_down, lambda i: write_row(i).start())
    for t in range(NT - 1):
        write(t).wait()
    for i in range(NI):
        write_row(i).wait()


def shards(tracers, courant_lon, courant_lat, level_counts, thick_source, eta_weights):
    dma, any_, vmem = pltpu.SemaphoreType.DMA, pl.BlockSpec(memory_space=pl.ANY), pl.BlockSpec(memory_space=pltpu.VMEM)
    tile9 = pltpu.VMEM((NI + 1, NK, 128), F32)
    pick = pltpu.VMEM((NK, 2 * SLOTS), F32)
    sums = pltpu.VMEM((NK + 8, 2 * NK), F32)
    thick, places = pltpu.VMEM((NK, NX), F32), pltpu.VMEM((NI + 1, NK, 128), jnp.int32)
    stage = pltpu.VMEM((2, NI, NK, SPAN), F32)

    def shape(v):
        return jax.ShapeDtypeStruct(v.shape, v.dtype)

    parts = pl.pallas_call(
        functools.partial(kernel, lax.axis_size("lat")),
        name="transport",
        out_shape=(jax.ShapeDtypeStruct((NT - 1, NI, NK, SPAN), F32), jax.ShapeDtypeStruct((ND, ROWS, 128), F32),
                   shape(pick), shape(thick), shape(places), shape(tile9), shape(tile9)),
        in_specs=[pl.BlockSpec(memory_space=pltpu.SMEM), any_, any_, any_, vmem, vmem],
        out_specs=(any_,) * 7,
        scratch_shapes=[
            pltpu.VMEM((NT, NS, NI, NX), F32),
            pltpu.VMEM((NT, 6, NS, NX), F32),
            pltpu.VMEM((NS, NI, NX), F32),
            pltpu.VMEM((NS, NI, NX), F32),
            pltpu.VMEM((NS, NX), F32),
            pltpu.VMEM((3, NS, NI, NX), F32),
            pltpu.VMEM((3, NS, NX), F32),
            pltpu.VMEM((3, NS, NI, NX), F32),
            pltpu.VMEM((3, NS, NX), F32),
            pltpu.VMEM((512, 512), jnp.bfloat16),
            pltpu.VMEM((9 * 112, 512), jnp.bfloat16),
            pltpu.VMEM((9 * 112, 512), F32),
            pltpu.VMEM((NS, NI, NX), F32),
            pltpu.VMEM((HELD, 3, NS, NX), F32),
            pltpu.VMEM((NT, ND, ROWS, 128), F32),
            pltpu.VMEM((ND, NT, ROWS, 128), F32),
            pick,
            sums,
            pltpu.VMEM((NK + 8, NX), F32),
            thick,
            places,
            tile9,
            tile9,
            pltpu.VMEM((2, NK, 128), F32),
            pltpu.VMEM((SLOTS, NX), F32),
            pltpu.VMEM((NK, NX), F32),
            pltpu.VMEM((NK + 8, NX), F32),
            pltpu.VMEM((NK + 8, 128), F32),
            stage,
            dma((NT,)),
            dma((2,)),
            dma((2,)),
            dma((NT, 6)),
            dma((NT, 6)),
            dma((HELD, 3)),
            dma((HELD, 3)),
            dma((NT, ND)),
            dma((NT, ND)),
            dma((NT,)),
            dma((5,)),
            dma((2,)),
        ],
        compiler_params=pltpu.CompilerParams(collective_id=0, has_side_effects=True, vmem_limit_bytes=VMEM1 << 20),
    )(level_counts, jnp.swapaxes(tracers, 1, 2), jnp.swapaxes(courant_lon, 0, 1), jnp.swapaxes(courant_lat, 0, 1),
      thick_source, eta_weights.reshape(1, NK))
    return pl.pallas_call(
        finish,
        name="finish",
        out_shape=jax.ShapeDtypeStruct((NT, NI, NK, SPAN), F32),
        in_specs=[any_] * 7,
        out_specs=any_,
        scratch_shapes=[
            pltpu.VMEM((ND, 1, ROWS, 128), F32), pick, sums, thick, places, tile9, tile9,
            pltpu.VMEM((SLOTS, NX), F32), pltpu.VMEM((NK, NX), F32), pltpu.VMEM((NK + 8, NX), F32), pltpu.VMEM((NK + 8, 128), F32),
            pltpu.VMEM((NT, NI, NK, SPAN), F32), dma((6,)), dma((NT - 1,)), dma((NT - 1,)), dma((NI,)),
        ],
        compiler_params=pltpu.CompilerParams(vmem_limit_bytes=VMEM2 << 20),
    )(*parts)


def solution(mesh):
    return jax.shard_map(
        shards,
        mesh=mesh,
        in_specs=(
            P(None, "lat", "lev", None),
            P("lat", "lev", None),
            P("lat", "lev", None),
            P(),
            P("lat", None, "lev"),
            P(),
        ),
        out_specs=P(None, "lat", None, "lev"),
        check_vma=False,
    )
```

```python
import functools
import jax
import jax.numpy as jnp
from jax import lax
from jax.experimental import pallas as pl
from jax.experimental.pallas import tpu as pltpu
from jax.sharding import PartitionSpec as P

MESH = pl.DeviceIdType.MESH
HI = lax.Precision.HIGHEST
F32 = jnp.float32
NT, NI, NS, NX, ND, NK = 8, 8, 13, 1152, 8, 72
SPAN = NX // ND
ROWS, HEAD = 120, 72
SLOTS = ND * NS
LINES = 3
HELD = -(-NT // LINES)
VMEM1, VMEM2 = 57, 57
MOVES = ((2, 1), (1, 1), (3, 1), (0, 1), (2, 0), (1, 0), (3, 0))


def gather(v, idx, axis):
    return jnp.take_along_axis(v, idx, axis=axis, mode="promise_in_bounds")


def iota(shape, axis):
    return lax.broadcasted_iota(jnp.int32, shape, axis)


def face_weights(c):
    m = jnp.abs(c)
    r = 1.0 - m
    cm = c * m
    return c * r * r * (1.0 / 12.0), cm * (3.0 - 2.0 * m), cm * r * (-1.0 / 12.0)


def flux_of(w, a, behind, ahead, a_behind, a_ahead):
    up = w[0] >= 0.0
    return w[0] * a + w[1] * jnp.where(up, behind, ahead) + w[2] * jnp.where(up, a_behind, a_ahead)


def face(q2, q1, q, qa):
    return 7.0 * (q1 + q) - (q2 + qa)


def edges(t, rows, xs, wedge, edge_s):
    def column(k, _):
        lanes = pl.ds(pl.multiple_of(k * 128, 128), 128)
        for lo, hi in ((0, 8), (8, NS)):
            n0, n1, n2, s3, s2, s1 = [rows[t, j, lo:hi, lanes] for j in range(6)]
            q0, q5, q6, q7 = [xs[t, lo:hi, j, lanes] for j in (0, 5, 6, 7)]
            a8 = face(q6, q7, n0, n1)
            edge_s[0, lo:hi, lanes] = face(s3, s2, s1, q0)
            edge_s[1, lo:hi, lanes] = a8
            edge_s[2, lo:hi, lanes] = flux_of(
                [wedge[j, lo:hi, lanes] for j in range(3)], a8, q7, n0, face(q5, q6, q7, n0), face(q7, n0, n1, n2))
        return 0

    lax.fori_loop(0, NX // 128, column, 0)


def stencil():
    p, c = iota((4 * 128, 4 * 128), 0), iota((4 * 128, 4 * 128), 1)
    u, kind = p & 127, c >> 7
    at = jnp.where(p < 256, u, jnp.where(u >= 64, u - 128, u + 128)) - (c & 127)
    near = at + jnp.where(kind == 1, 1, jnp.where(kind == 2, -1, 0))
    value = jnp.where((near == -1) | (near == 0), 7.0, jnp.where((near == -2) | (near == 1), -1.0, 0.0))
    return jnp.where(kind == 3, jnp.where(at == -1, 1.0, 0.0), value).astype(jnp.bfloat16)


def halves(v):
    hi = v.astype(jnp.bfloat16)
    return hi, (v - hi.astype(F32)).astype(jnp.bfloat16)


def lane_stencil(t, xs, sten, taps, faces):
    nk = NX // 128
    pad = jnp.zeros((8, 128), F32)
    lane = iota((NS * NI, 128), 1)
    for k in range(nk):
        col = [xs[t, :, :, 128 * j:128 * j + 128].reshape(NS * NI, 128) for j in ((k + nk - 1) % nk, k, (k + 1) % nk)]
        both = halves(jnp.concatenate([col[1], pad], axis=0)) + halves(
            jnp.concatenate([jnp.where(lane >= 64, col[0], col[2]), pad], axis=0))
        for j, piece in enumerate(both):
            taps[112 * k:112 * k + 112, 128 * j:128 * j + 128] = piece
    faces[...] = jnp.dot(taps[...], sten[...], preferred_element_type=F32)


def longitude(t, xs, wlon, sten, taps, faces, part):
    lane = iota((8, 128), 1)
    nk = NX // 128
    lane_stencil(t, xs, sten, taps, faces)
    for l in range(NS):
        flux = []
        for k in range(nk):
            a, a_west, a_east, west = [faces[112 * k + 8 * l:112 * k + 8 * l + 8, 128 * j:128 * j + 128] for j in range(4)]
            flux.append(flux_of([wlon[j, l, :, 128 * k:128 * k + 128] for j in range(3)], a, west,
                                xs[t, l, :, 128 * k:128 * k + 128], a_west, a_east))
        turned = [pltpu.roll(f, 127, 1) for f in flux]
        for k in range(nk):
            flux_east = jnp.where(lane < 127, turned[k], turned[(k + 1) % nk])
            part[l, :, 128 * k:128 * k + 128] = xs[t, l, :, 128 * k:128 * k + 128] - (flux_east - flux[k])


def latitude(t, levels, xs, rows, edge_s, wlat, part, send):
    sub, lane = iota((8, 128), 0), iota((8, 128), 1)
    first, second, last = sub == 0, sub == 1, sub == 7

    def wide(ref, l, k):
        return jnp.broadcast_to(ref[l:l + 1, 128 * k:128 * k + 128], (8, 128))

    for l in levels:
        h = []
        for k in range(NX // 128):
            q = xs[t, l, :, 128 * k:128 * k + 128]
            s1 = wide(rows.at[t, 5], l, k)
            q1 = jnp.where(first, s1, pltpu.roll(q, 1, 0))
            q2 = jnp.where(first, wide(rows.at[t, 4], l, k), jnp.where(second, s1, pltpu.roll(q, 2, 0)))
            qa = jnp.where(last, wide(rows.at[t, 0], l, k), pltpu.roll(q, 7, 0))
            b = face(q2, q1, q, qa)
            b1 = jnp.where(first, wide(edge_s.at[0], l, k), pltpu.roll(b, 1, 0))
            ba = jnp.where(last, wide(edge_s.at[1], l, k), pltpu.roll(b, 7, 0))
            g = flux_of([wlat[j, l, :, 128 * k:128 * k + 128] for j in range(3)], b, q1, q, b1, ba)
            ga = jnp.where(last, wide(edge_s.at[2], l, k), pltpu.roll(g, 7, 0))
            h.append(part[l, :, 128 * k:128 * k + 128] - (ga - g))
        main, tail, at = 8 * l + (8 if l >= 8 else 0), 112 if l >= 8 else 64, 16 * (l % 8)
        for e in range(ND):
            send[t, e, main:main + 8, :] = jnp.where(lane >= 16 * e, h[e], h[e + 1]) if e else h[0]
            turn = (128 - 16 * e + at) % 128
            piece = pltpu.roll(h[e + 1], turn, 1) if turn else h[e + 1]
            send[t, e, tail:tail + 8, at:at + 16] = piece[:, at:at + 16]


def split(v, parts):
    out = []
    for _ in range(parts):
        p = v.astype(jnp.bfloat16)
        out.append(p)
        v = v - p.astype(F32)
    return jnp.concatenate(out, axis=0)


def zero_one(mask, parts):
    return jnp.concatenate([jnp.where(mask, 1.0, 0.0)] * parts, axis=1)


def below_sum():
    return zero_one(iota((NK + 8, NK), 1) < iota((NK + 8, NK), 0), 2)


def mul(m, v):
    return jnp.dot(m.astype(jnp.bfloat16), v, preferred_element_type=F32)


def prep(lev, cnt_ref, thick_ref, eta_ref, pick_s, sum_s, su_s, th_s, idx_s, dt_s, rt_s, fr_s):
    for i in range(NI):
        th_s[:, 128 * i:128 * i + 128] = pltpu.roll(thick_ref[i, :, 0:128], lax.rem(16 * lev, 128), 1)
        th_s[:, NX - 128 + 16 * i:NX - 112 + 16 * i] = thick_ref[i, :, 128:SPAN]
    level, slot = iota((NK, SLOTS), 0), iota((NK, SLOTS), 1)
    source = jnp.zeros((NK, SLOTS), jnp.int32)
    start = jnp.int32(0)
    for d in range(ND):
        c = cnt_ref[d]
        source = jnp.where((level >= start) & (level < start + c), level - start + NS * d, source)
        start = start + c
    pick_s[...] = zero_one(source == slot, 2)
    sum_s[...] = below_sum()
    r72, l72 = iota((NK, NK), 0), iota((NK, NK), 1)
    eb = jnp.broadcast_to(eta_ref[...], (NK, NK))
    tot = jnp.sum(eb, axis=1, keepdims=True)
    cum = jnp.sum(jnp.where(l72 <= r72, eb, 0.0), axis=1, keepdims=True)
    own = jnp.sum(jnp.where(l72 == r72, eb, 0.0), axis=1, keepdims=True)
    fr_s[0] = jnp.broadcast_to(cum / tot, (NK, 128))
    fr_s[1] = jnp.broadcast_to(own / tot, (NK, 128))
    su_s[...] = mul(zero_one(iota((NK + 8, NK), 1) < iota((NK + 8, NK), 0), 3), split(th_s[...], 3))

    def one(ct, _):
        lanes = pl.ds(pl.multiple_of(ct * 128, 128), 128)
        ps = jnp.broadcast_to(su_s[NK:NK + 1, lanes], (8, 128))
        for tb in range(NK // 8):
            at = slice(8 * tb, 8 * tb + 8)
            t = ps * fr_s[0, at, :]
            rt_s[ct, at, :] = 1.0 / (ps * fr_s[1, at, :])
            n = jnp.zeros((8, 128), jnp.int32)
            for r in range(NK):
                n = jnp.where(jnp.broadcast_to(su_s[r + 1:r + 2, lanes], (8, 128)) <= t, r + 1, n)
            loc, vb = n & 7, n >> 3
            g = ps
            gh = jnp.zeros((8, 128), F32)
            for v in range(NK // 8):
                hit = vb == v
                g = jnp.where(hit, gather(su_s[8 * v:8 * v + 8, lanes], loc, 0), g)
                gh = jnp.where(hit, gather(th_s[8 * v:8 * v + 8, lanes], loc, 0), gh)
            idx_s[ct, at, :] = n
            dt_s[ct, at, :] = jnp.clip(t - g, 0.0, gh)
        return 0

    lax.fori_loop(0, NI + 1, one, 0)


def block_turn(p):
    r, l = iota((8, 128), 0), iota((8, 128), 1)
    p = gather(p, (l + 16 * r) & 127, 1)
    p = gather(p, (r - (l >> 4)) & 7, 0)
    return gather(p, ((16 * r - (l & 112)) & 127) + (l & 15), 1)


def remap_tracer(lev, t, slot, recv, stage, pick_s, sum_s, th_s, idx_s, dt_s, rt_s, s_s, q_s, c_s, f_s, ready=None, before=None, after=None):
    for d in range(ND):
        a, b = slice(NS * d, NS * d + 8), slice(NS * d + 8, NS * d + NS)
        for ct in range(NI):
            lanes = slice(128 * ct, 128 * ct + 128)
            s_s[a, lanes] = recv[d, t, pl.ds(ct, 8, stride=8), :]
            s_s[b, lanes] = recv[d, t, pl.ds(72 + ct, NS - 8, stride=8), :]
        s_s[a, NX - 128:] = block_turn(recv[d, t, 64:72, :])
        s_s[b, NX - 128:] = block_turn(recv[d, t, 112:120, :])[:NS - 8]
    q_s[...] = mul(pick_s[...], split(s_s[...], 2))
    c_s[...] = mul(sum_s[...], split(q_s[...] * th_s[...], 2))
    f_s[0:8, :] = jnp.zeros((8, 128), F32)
    if ready is not None:
        ready()

    def tile(ct):
        lanes = pl.ds(ct * 128, 128) if isinstance(ct, int) else pl.ds(pl.multiple_of(ct * 128, 128), 128)
        total = jnp.broadcast_to(c_s[NK:NK + 1, lanes], (8, 128))
        for tb in range(NK // 8):
            at = slice(8 * tb, 8 * tb + 8)
            n = idx_s[ct, at, :]
            loc, vb = n & 7, n >> 3
            gc = total
            gq = jnp.zeros((8, 128), F32)
            for v in range(NK // 8):
                hit = vb == v
                gc = jnp.where(hit, gather(c_s[8 * v:8 * v + 8, lanes], loc, 0), gc)
                gq = jnp.where(hit, gather(q_s[8 * v:8 * v + 8, lanes], loc, 0), gq)
            f_s[8 + 8 * tb:16 + 8 * tb, :] = gc + dt_s[ct, at, :] * gq
        return (f_s[8:80, :] - f_s[7:79, :]) * rt_s[ct]

    res = tile(NI)
    for i in range(NI):
        stage[slot, i, :, 128:SPAN] = res[:, 16 * i:16 * i + 16]

    def main(ct, _):
        if before is not None:
            before(ct)
        stage[slot, ct, :, 0:128] = pltpu.roll(tile(ct), lax.rem(128 - 16 * lev, 128), 1)
        if after is not None:
            after(ct)
        return 0

    lax.fori_loop(0, NI, main, 0)


def kernel(lat_axis, cnt_ref, x_hbm, clon_hbm, clat_hbm, thick_ref, eta_ref, done, late, pick_o, th_o, idx_o, dt_o, rt_o,
           xs, rows, clon, clat, cnorth, wlat, wedge, wlon, edge_s, sten, taps, faces, part, held, send, recv,
           pick_s, sum_s, su_s, th_s, idx_s, dt_s, rt_s, fr_s, s_s, q_s, c_s, f_s, stage,
           x_sem, c_sem, esem, hsend, hrecv, held_sem, rest_sem, ssem, rsem, lsem, psem, osem):
    lat, lev = lax.axis_index("lat"), lax.axis_index("lev")
    has_south, has_north = lat > 0, lat < lat_axis - 1

    small = [pltpu.make_async_copy(clat_hbm, clat, c_sem.at[0]), pltpu.make_async_copy(clon_hbm, clon, c_sem.at[1])]
    loads = [pltpu.make_async_copy(x_hbm.at[t], xs.at[t], x_sem.at[t]) for t in range(NT)]
    small[0].start()
    small[1].start()
    loads[0].start()

    def peer(k):
        y, z = MOVES[k - 1]
        return lax.rem(lev // 2 + y, 4) * 2 + lax.rem(lev + z, 2)

    bar = pltpu.get_barrier_semaphore()
    for k in range(1, ND):
        pl.semaphore_signal(bar, inc=1, device_id=(lat, peer(k)), device_id_type=MESH)

    @pl.when(has_south)
    def _():
        pl.semaphore_signal(bar, inc=1, device_id=(lat - 1, lev), device_id_type=MESH)

    @pl.when(has_north)
    def _():
        pl.semaphore_signal(bar, inc=1, device_id=(lat + 1, lev), device_id_type=MESH)

    below, above = lat_axis // 2 - 1, lat_axis // 2
    up_relays = [lat_axis - 2 * i for i in range(1, LINES)]
    down_relays = [2 * i - 1 for i in range(1, LINES)]

    def one_of(places):
        return functools.reduce(jnp.logical_or, [lat == p for p in places])

    def greet(here, places):
        @pl.when(here)
        def _():
            for p in places:
                pl.semaphore_signal(bar, inc=1, device_id=(p, lev), device_id_type=MESH)

    is_up, is_down = one_of(up_relays), one_of(down_relays)
    greet(lat == above, up_relays)
    greet(lat == below, down_relays)
    greet(is_up, [below])
    greet(is_down, [above])
    others = (jnp.where(has_south, 1, 0) + jnp.where(has_north, 1, 0) + jnp.where(is_up, 1, 0) + jnp.where(is_down, 1, 0)
              + jnp.where(lat == above, LINES - 1, 0) + jnp.where(lat == below, LINES - 1, 0))
    pl.semaphore_wait(bar, ND - 1 + others)

    def edge_copy():
        return pltpu.make_async_remote_copy(clat_hbm.at[:, 0, :], cnorth, esem.at[0], esem.at[1],
                                            device_id=(lat - 1, lev), device_id_type=MESH)

    def to_south(t, j):
        return pltpu.make_async_remote_copy(x_hbm.at[t, :, j, :], rows.at[t, j], hsend.at[t, j], hrecv.at[t, j],
                                            device_id=(lat - 1, lev), device_id_type=MESH)

    def to_north(t, j):
        return pltpu.make_async_remote_copy(x_hbm.at[t, :, 2 + j, :], rows.at[t, j], hsend.at[t, j], hrecv.at[t, j],
                                            device_id=(lat + 1, lev), device_id_type=MESH)

    @pl.when(has_south)
    def _():
        edge_copy().start()

    def up_leg(t, j):
        slot = t // LINES
        return pltpu.make_async_remote_copy(x_hbm.at[t, :, 5 + j, :], held.at[slot, j], hsend.at[t, 3 + j], held_sem.at[slot, j],
                                            device_id=(lat_axis - 2 * (t % LINES), lev), device_id_type=MESH)

    def down_leg(t, j):
        slot = t // LINES
        return pltpu.make_async_remote_copy(x_hbm.at[t, :, j, :], held.at[slot, j], hsend.at[t, j], held_sem.at[slot, j],
                                            device_id=(2 * (t % LINES) - 1, lev), device_id_type=MESH)

    def up_rest(t, j):
        return pltpu.make_async_remote_copy(held.at[t // LINES, j], rows.at[t, 3 + j], rest_sem.at[t // LINES, j], hrecv.at[t, 3 + j],
                                            device_id=(above, lev), device_id_type=MESH)

    def down_rest(t, j):
        return pltpu.make_async_remote_copy(held.at[t // LINES, j], rows.at[t, j], rest_sem.at[t // LINES, j], hrecv.at[t, j],
                                            device_id=(below, lev), device_id_type=MESH)

    def relay(t):
        line = lax.rem(t, LINES)

        @pl.when((t < NT) & (line > 0) & (lat == lat_axis - 2 * line))
        def _():
            for j in range(3):
                up_leg(t, j).wait_recv()
                up_rest(t, j).start()

        @pl.when((t < NT) & (line > 0) & (lat == 2 * line - 1))
        def _():
            for j in range(3):
                down_leg(t, j).wait_recv()
                down_rest(t, j).start()

    for t in range(NT):
        straight = t % LINES == 0

        @pl.when(has_south if straight else has_south & (lat != above))
        def _():
            for j in range(3):
                to_south(t, j).start()

        @pl.when(has_north if straight else has_north & (lat != below))
        def _():
            for j in range(3, 6):
                to_north(t, j).start()

        if not straight:
            @pl.when(lat == above)
            def _():
                for j in range(3):
                    down_leg(t, j).start()

            @pl.when(lat == below)
            def _():
                for j in range(3):
                    up_leg(t, j).start()

        if t > 0:
            loads[t].start()

    @pl.when(lat == 0)
    def _():
        rows[:, 3:6] = jnp.zeros((NT, 3, NS, NX), F32)

    @pl.when(lat == lat_axis - 1)
    def _():
        rows[:, 0:3] = jnp.zeros((NT, 3, NS, NX), F32)
        cnorth[...] = jnp.zeros_like(cnorth)

    sten[...] = stencil()
    small[0].wait()
    small[1].wait()

    def weigh(l, _):
        for k, w in enumerate(face_weights(clat[l])):
            wlat[k, l] = w
        for k, w in enumerate(face_weights(clon[l])):
            wlon[k, l] = w
        return 0

    lax.fori_loop(0, NS, weigh, 0)

    def clear(t, _):
        for e in range(ND):
            send[t, e, 112:120, :] = jnp.zeros((8, 128), F32)
        return 0

    lax.fori_loop(0, NT, clear, 0)

    @pl.when(has_north)
    def _():
        edge_copy().wait_recv()

    for k, w in enumerate(face_weights(cnorth[...])):
        wedge[k] = w

    def across(t, k, last=False):
        e = peer(k)
        return pltpu.make_async_remote_copy(send.at[t, e], late.at[lev] if last else recv.at[lev, t], ssem.at[t, k], rsem.at[t, lev],
                                            device_id=(lat, e), device_id_type=MESH)

    def across_part(t, k, lo, hi):
        e = peer(k)
        return pltpu.make_async_remote_copy(send.at[t, e, lo:hi], recv.at[lev, t, lo:hi], ssem.at[t, k], rsem.at[t, lev],
                                            device_id=(lat, e), device_id_type=MESH)

    def own(t, last=False):
        return pltpu.make_async_copy(send.at[t, lev], late.at[lev] if last else recv.at[lev, t], lsem.at[t])

    def forward(t, _):
        pltpu.make_async_copy(x_hbm.at[t], xs.at[t], x_sem.at[t]).wait()
        longitude(t, xs, wlon, sten, taps, faces, part)
        relay(t + 1)

        bent = lax.rem(t, LINES) > 0
        from_above, from_below = bent & (lat == below), bent & (lat == above)

        @pl.when(has_north & ~from_above)
        def _():
            for j in range(3):
                to_south(t, j).wait_recv()

        @pl.when(has_south & ~from_below)
        def _():
            for j in range(3, 6):
                to_north(t, j).wait_recv()

        @pl.when(from_above)
        def _():
            for j in range(3):
                down_rest(t, j).wait_recv()

        @pl.when(from_below)
        def _():
            for j in range(3):
                up_rest(t, j).wait_recv()

        edges(t, rows, xs, wedge, edge_s)
        latitude(t, range(8), xs, rows, edge_s, wlat, part, send)

        @pl.when(t == 0)
        def _():
            for k in range(1, ND):
                across_part(t, k, 0, HEAD).start()

        latitude(t, range(8, NS), xs, rows, edge_s, wlat, part, send)

        @pl.when(t == 0)
        def _():
            for k in range(1, ND):
                across_part(t, k, HEAD, ROWS).start()
            own(t).start()

        @pl.when((t > 0) & (t < NT - 1))
        def _():
            for k in range(1, ND):
                across(t, k).start()
            own(t).start()

        @pl.when(t == NT - 1)
        def _():
            for k in range(1, ND):
                across(t, k, True).start()
            own(t, True).start()
        return 0

    lax.fori_loop(0, NT, forward, 0)

    prep(lev, cnt_ref, thick_ref, eta_ref, pick_s, sum_s, su_s, th_s, idx_s, dt_s, rt_s, fr_s)

    kept = [pltpu.make_async_copy(v, o, psem.at[i]) for i, (v, o) in enumerate(
        ((pick_s, pick_o), (th_s, th_o), (idx_s, idx_o), (dt_s, dt_o), (rt_s, rt_o)))]
    for c in kept:
        c.start()

    def put(t, slot):
        return pltpu.make_async_copy(stage.at[slot], done.at[t], osem.at[slot])

    def settle(t, _):
        own(t).wait()
        for k in range(1, ND):
            src = peer(k)
            pltpu.make_async_remote_copy(send.at[t, src], recv.at[src, t], ssem.at[t, k], rsem.at[t, src],
                                         device_id=(lat, src), device_id_type=MESH).wait_recv()
        slot = lax.rem(t, 2)

        @pl.when(t >= 2)
        def _():
            put(t - 2, slot).wait()

        remap_tracer(lev, t, slot, recv, stage, pick_s, sum_s, th_s, idx_s, dt_s, rt_s, s_s, q_s, c_s, f_s)
        put(t, slot).start()
        return 0

    lax.fori_loop(0, NT - 1, settle, 0)
    put(NT - 3, (NT - 3) % 2).wait()
    put(NT - 2, (NT - 2) % 2).wait()
    for c in kept:
        c.wait()
    own(NT - 1, True).wait()
    for k in range(1, ND):
        src = peer(k)
        pltpu.make_async_remote_copy(send.at[NT - 1, src], late.at[src], ssem.at[NT - 1, k], rsem.at[NT - 1, src],
                                     device_id=(lat, src), device_id_type=MESH).wait_recv()

    def drain(t, _):
        for k in range(1, ND):
            across(t, k).wait_send()

        @pl.when(has_south)
        def _():
            for j in range(3):
                to_south(t, j).wait_send()

        @pl.when(has_north)
        def _():
            for j in range(3, 6):
                to_north(t, j).wait_send()
        return 0

    lax.fori_loop(0, NT, drain, 0)

    for t in range(NT):
        line = t % LINES
        if line:
            @pl.when((lat == lat_axis - 2 * line) | (lat == 2 * line - 1))
            def _():
                for j in range(3):
                    up_rest(t, j).wait_send()

    @pl.when(has_south)
    def _():
        edge_copy().wait_send()


def finish(done, late, pick_h, th_h, idx_h, dt_h, rt_h, out, recv, pick_s, sum_s, th_s, idx_s, dt_s, rt_s, s_s, q_s, c_s, f_s, stage,
           isem, csem, osem, wsem):
    loads = [pltpu.make_async_copy(h, v, isem.at[i]) for i, (h, v) in enumerate(
        ((late, recv.at[:, 0]), (pick_h, pick_s), (th_h, th_s), (idx_h, idx_s), (dt_h, dt_s), (rt_h, rt_s)))]

    def fetch(t):
        return pltpu.make_async_copy(done.at[t], stage.at[t], csem.at[t])

    def write(t):
        return pltpu.make_async_copy(stage.at[t], out.at[t], osem.at[t])

    def lay_down(t):
        @pl.when(t < NT - 1)
        def _():
            fetch(t).wait()
            write(t).start()

    def write_row(i):
        return pltpu.make_async_copy(stage.at[NT - 1, i], out.at[NT - 1, i], wsem.at[i])

    def ready():
        for c in loads[3:]:
            c.wait()

    for c in loads:
        c.start()
    for t in range(NT - 1):
        fetch(t).start()
    sum_s[...] = below_sum()
    for c in loads[:3]:
        c.wait()
    remap_tracer(lax.axis_index("lev"), 0, NT - 1, recv, stage, pick_s, sum_s, th_s, idx_s, dt_s, rt_s, s_s, q_s, c_s, f_s,
                 ready, lay_down, lambda i: write_row(i).start())
    for t in range(NT - 1):
        write(t).wait()
    for i in range(NI):
        write_row(i).wait()


def shards(tracers, courant_lon, courant_lat, level_counts, thick_source, eta_weights):
    dma, any_, vmem = pltpu.SemaphoreType.DMA, pl.BlockSpec(memory_space=pl.ANY), pl.BlockSpec(memory_space=pltpu.VMEM)
    tile9 = pltpu.VMEM((NI + 1, NK, 128), F32)
    pick = pltpu.VMEM((NK, 2 * SLOTS), F32)
    sums = pltpu.VMEM((NK + 8, 2 * NK), F32)
    thick, places = pltpu.VMEM((NK, NX), F32), pltpu.VMEM((NI + 1, NK, 128), jnp.int32)
    stage = pltpu.VMEM((2, NI, NK, SPAN), F32)

    def shape(v):
        return jax.ShapeDtypeStruct(v.shape, v.dtype)

    parts = pl.pallas_call(
        functools.partial(kernel, lax.axis_size("lat")),
        name="transport",
        out_shape=(jax.ShapeDtypeStruct((NT - 1, NI, NK, SPAN), F32), jax.ShapeDtypeStruct((ND, ROWS, 128), F32),
                   shape(pick), shape(thick), shape(places), shape(tile9), shape(tile9)),
        in_specs=[pl.BlockSpec(memory_space=pltpu.SMEM), any_, any_, any_, vmem, vmem],
        out_specs=(any_,) * 7,
        scratch_shapes=[
            pltpu.VMEM((NT, NS, NI, NX), F32),
            pltpu.VMEM((NT, 6, NS, NX), F32),
            pltpu.VMEM((NS, NI, NX), F32),
            pltpu.VMEM((NS, NI, NX), F32),
            pltpu.VMEM((NS, NX), F32),
            pltpu.VMEM((3, NS, NI, NX), F32),
            pltpu.VMEM((3, NS, NX), F32),
            pltpu.VMEM((3, NS, NI, NX), F32),
            pltpu.VMEM((3, NS, NX), F32),
            pltpu.VMEM((512, 512), jnp.bfloat16),
            pltpu.VMEM((9 * 112, 512), jnp.bfloat16),
            pltpu.VMEM((9 * 112, 512), F32),
            pltpu.VMEM((NS, NI, NX), F32),
            pltpu.VMEM((HELD, 3, NS, NX), F32),
            pltpu.VMEM((NT, ND, ROWS, 128), F32),
            pltpu.VMEM((ND, NT, ROWS, 128), F32),
            pick,
            sums,
            pltpu.VMEM((NK + 8, NX), F32),
            thick,
            places,
            tile9,
            tile9,
            pltpu.VMEM((2, NK, 128), F32),
            pltpu.VMEM((SLOTS, NX), F32),
            pltpu.VMEM((NK, NX), F32),
            pltpu.VMEM((NK + 8, NX), F32),
            pltpu.VMEM((NK + 8, 128), F32),
            stage,
            dma((NT,)),
            dma((2,)),
            dma((2,)),
            dma((NT, 6)),
            dma((NT, 6)),
            dma((HELD, 3)),
            dma((HELD, 3)),
            dma((NT, ND)),
            dma((NT, ND)),
            dma((NT,)),
            dma((5,)),
            dma((2,)),
        ],
        compiler_params=pltpu.CompilerParams(collective_id=0, has_side_effects=True, vmem_limit_bytes=VMEM1 << 20),
    )(level_counts, jnp.swapaxes(tracers, 1, 2), jnp.swapaxes(courant_lon, 0, 1), jnp.swapaxes(courant_lat, 0, 1),
      thick_source, eta_weights.reshape(1, NK))
    return pl.pallas_call(
        finish,
        name="finish",
        out_shape=jax.ShapeDtypeStruct((NT, NI, NK, SPAN), F32),
        in_specs=[any_] * 7,
        out_specs=any_,
        scratch_shapes=[
            pltpu.VMEM((ND, 1, ROWS, 128), F32), pick, sums, thick, places, tile9, tile9,
            pltpu.VMEM((SLOTS, NX), F32), pltpu.VMEM((NK, NX), F32), pltpu.VMEM((NK + 8, NX), F32), pltpu.VMEM((NK + 8, 128), F32),
            pltpu.VMEM((NT, NI, NK, SPAN), F32), dma((6,)), dma((NT - 1,)), dma((NT - 1,)), dma((NI,)),
        ],
        compiler_params=pltpu.CompilerParams(vmem_limit_bytes=VMEM2 << 20),
    )(*parts)


def solution(mesh):
    return jax.shard_map(
        shards,
        mesh=mesh,
        in_specs=(
            P(None, "lat", "lev", None),
            P("lat", "lev", None),
            P("lat", "lev", None),
            P(),
            P("lat", None, "lev"),
            P(),
        ),
        out_specs=P(None, "lat", None, "lev"),
        check_vma=False,
    )
```
